32 devices in a mesh: tile: 8 (over z, x), fsdp: 4 (over y, core).
Axes of the slice: x: 2, y: 2, z: 4, core: 2. Of those that a mesh axis runs over, the one named last changes fastest.
Arguments:
- fields: bfloat16 [4, 32, 64, 512], P('fsdp', None, 'tile'), may hold values from -6 to 6
- seam_shift: int32 [8, 2], P('tile'), may hold values from -4 to 4
- kernel: float32 [49, 512], replicated, may hold values from -0.875 to 0.875
- gain: float32 [512], replicated, may hold values from 0.3 to 3
- w_in: bfloat16 [512, 2048], P(None, 'fsdp'), may hold values from -0.25 to 0.25
- w_out: bfloat16 [2048, 512], P('fsdp'), may hold values from -0.125 to 0.125
- cotangent: bfloat16 [4, 32, 64, 512], P('fsdp', None, 'tile'), may hold values from -6 to 6
Outputs:
- mixed: bfloat16 [4, 32, 64, 512], P('fsdp', None, 'tile')
- field_grad: bfloat16 [4, 32, 64, 512], P('fsdp', None, 'tile')
- kernel_grad: float32 [49, 512], replicated
- gain_grad: float32 [512], replicated
- w_in_grad: float32 [512, 2048], P(None, 'fsdp')
- w_out_grad: float32 [2048, 512], P('fsdp')
The draws below stay inside these ranges and needn't reach their ends.
Inputs may be any that keep to these rules, and one draw needn't show every extreme that they name: `seam_shift`: offset added to the row index of cells taken across a tile's west (column 0) or east (column 1) seam.
All inputs are finite; a program needn't handle non-finite values.
Results may differ from the reference program's by a relative error of at most 0.0095.
Values may be sent and summed in bfloat16 or wider, within the bound.
A program may use at most 128 MiB of HBM per device.

```python
import math
import jax
import jax.numpy as jnp
from jax import lax

C = 512
HID = 2048
TAPS = 49
LAT = 32
LON_DEV = 8
SAMPLES = 4
TILES = 8
LON = 64
CELLS = 8192


def touch_ends(drawn, stream_key, smallest, largest):
    shape = drawn.shape
    index_at = [jax.random.randint(jax.random.fold_in(stream_key, axis), (), 0, shape[axis]) for axis in range(len(shape))]
    drawn = drawn.at[tuple(index_at)].set(smallest)
    longest = shape.index(max(shape))
    index_at[longest] = (index_at[longest] + 1) % shape[longest]
    return drawn.at[tuple(index_at)].set(largest)


def block_scale(own_key, dims, pieces, low, high):
    level = 1.0
    for axis_at, parts in pieces:
        heights = jax.random.uniform(jax.random.fold_in(jax.random.fold_in(own_key, 6), axis_at), (parts,), jnp.float32, low / len(pieces), high / len(pieces))
        level = level * jnp.repeat(jnp.exp(heights), dims[axis_at] // parts).reshape((-1,) + (1,) * (len(dims) - 1 - axis_at))
    return level


def centred(rng, dims, deviation, most, cuts=(), kind=jnp.bfloat16):
    entries = jax.random.normal(rng, dims, jnp.float32) * deviation
    if len(cuts) > 0:
        entries = block_scale(rng, dims, cuts, -0.22, 0.18) * entries
    return jnp.clip(entries, min=-most, max=most).astype(kind)


def setup_inputs(seed: int = 0) -> dict:
    streams_of = jax.random.split(jax.random.key(seed), 8)
    fields = centred(streams_of[0], (SAMPLES, LAT, LON, C), 1.0, 6.0, ((0, 4), (2, 8)))
    seam_shift = touch_ends(jax.random.randint(streams_of[1], (TILES, 2), -4, 5), jax.random.fold_in(streams_of[1], 1), -4, 4).astype(jnp.int32)
    kernel = centred(streams_of[2], (TAPS, C), TAPS ** -0.5, 0.875, (), jnp.float32)
    gain = jnp.clip(jnp.exp(jax.random.uniform(streams_of[3], (C,), jnp.float32, math.log(0.3), math.log(3.0))), 0.3, 3.0)
    w_in = centred(streams_of[4], (C, HID), C ** -0.5, 0.25, ((1, 4),))
    w_out = centred(streams_of[5], (HID, C), HID ** -0.5, 0.125, ((0, 4),))
    cotangent = centred(streams_of[6], (SAMPLES, LAT, LON, C), 1.0, 6.0, ((0, 4), (2, 8)))
    return dict(fields=fields, seam_shift=seam_shift, kernel=kernel, gain=gain, w_in=w_in, w_out=w_out, cotangent=cotangent)


eps = 1e-06
inv_root2 = 0.7071067811865476
inv_root_tau = 0.3989422804014327

def gelu(value):
    return value * 0.5 * (1.0 + lax.erf(value * inv_root2))

def gelu_slope(value):
    return 0.5 * (1.0 + lax.erf(value * inv_root2)) + value * inv_root_tau * jnp.exp(-0.5 * value * value)

def shift_rows(strip, offsets):
    height = strip.shape[0]
    rows = jnp.arange(height, dtype=jnp.int32)[:, None] + offsets[None, :].astype(jnp.int32)
    valid = (rows >= 0) & (rows < height)
    clipped = jnp.clip(rows, 0, height - 1).astype(jnp.int32)
    index = jnp.broadcast_to(clipped[:, :, None, None], strip.shape)
    taken = jnp.take_along_axis(strip, index, axis=0)
    return jnp.where(valid[:, :, None, None], taken, jnp.zeros_like(taken))

def extend(plane, seam_shift):
    tiles = plane.reshape(LAT, TILES, LON_DEV, C)
    west = shift_rows(jnp.roll(tiles, 1, axis=1)[:, :, LON_DEV - 3:], seam_shift[:, 0])
    east = shift_rows(jnp.roll(tiles, -1, axis=1)[:, :, :3], seam_shift[:, 1])
    joined = jnp.concatenate([west, tiles, east], axis=2)
    return jnp.pad(joined, ((3, 3), (0, 0), (0, 0), (0, 0)))

def depthwise(padded, kernel):
    total = jnp.zeros((LAT, TILES, LON_DEV, C), jnp.float32)
    for row in range(7):
        for col in range(7):
            total = total + padded[row:row + LAT, :, col:col + LON_DEV, :] * kernel[7 * row + col]
    return total

def reference(fields, seam_shift, kernel, gain, w_in, w_out, cotangent):

    def tile_step(carry, inputs):
        sum_in, sum_out, sum_gain = carry
        mixed_tile, plane_tile, back_tile = inputs
        rows = mixed_tile.reshape(LAT * LON_DEV, C)
        mean = lax.optimization_barrier(jnp.mean(rows, axis=-1, keepdims=True))
        centered = rows - mean
        rstd = lax.rsqrt(lax.optimization_barrier(jnp.mean(centered * centered, axis=-1, keepdims=True)) + eps)
        normed = centered * rstd
        scaled = (normed * gain).astype(jnp.bfloat16)
        pre = jnp.dot(scaled, w_in, preferred_element_type=jnp.float32)
        hidden = gelu(pre).astype(jnp.bfloat16)
        branch = jnp.dot(hidden, w_out, preferred_element_type=jnp.float32)
        residual = plane_tile.reshape(LAT * LON_DEV, C).astype(jnp.float32)
        output = (residual + branch).astype(jnp.bfloat16).reshape(LAT, LON_DEV, C)
        back = back_tile.reshape(LAT * LON_DEV, C)
        d_hidden = lax.dot_general(back, w_out, (((1,), (1,)), ((), ())), preferred_element_type=jnp.float32)
        d_pre = (d_hidden * gelu_slope(pre)).astype(jnp.bfloat16)
        term_out = lax.dot_general(hidden, back, (((0,), (0,)), ((), ())), preferred_element_type=jnp.float32)
        term_in = lax.dot_general(scaled, d_pre, (((0,), (0,)), ((), ())), preferred_element_type=jnp.float32)
        d_scaled = lax.dot_general(d_pre, w_in, (((1,), (1,)), ((), ())), preferred_element_type=jnp.float32)
        term_gain = lax.optimization_barrier(jnp.sum(d_scaled * normed, axis=0))
        d_normed = d_scaled * gain
        d_rows = (d_normed - lax.optimization_barrier(jnp.mean(d_normed, axis=-1, keepdims=True)) - normed * lax.optimization_barrier(jnp.mean(d_normed * normed, axis=-1, keepdims=True))) * rstd
        return ((sum_in + term_in, sum_out + term_out, sum_gain + term_gain), (output, d_rows.reshape(LAT, LON_DEV, C)))

    def by_tile(plane):
        return jnp.moveaxis(plane.reshape(LAT, TILES, LON_DEV, C), 1, 0)

    def sample_step(carry, inputs):
        sum_in, sum_out, sum_gain, sum_kernel = carry
        plane, back_plane = inputs
        plane32 = plane.astype(jnp.float32)
        mixed_in, pullback = jax.vjp(lambda field, taps: depthwise(extend(field, seam_shift), taps), plane32, kernel)
        (sum_in, sum_out, sum_gain), (out_tiles, d_tiles) = lax.scan(tile_step, (sum_in, sum_out, sum_gain), (jnp.moveaxis(mixed_in, 1, 0), by_tile(plane), by_tile(back_plane)))
        d_plane, d_kernel = pullback(jnp.moveaxis(d_tiles, 0, 1))
        mixed_plane = jnp.moveaxis(out_tiles, 0, 1).reshape(LAT, LON, C)
        grad_plane = (back_plane.astype(jnp.float32) + d_plane).astype(jnp.bfloat16)
        return ((sum_in, sum_out, sum_gain, sum_kernel + d_kernel), (mixed_plane, grad_plane))
    start = (jnp.zeros((C, HID), jnp.float32), jnp.zeros((HID, C), jnp.float32), jnp.zeros((C,), jnp.float32), jnp.zeros((TAPS, C), jnp.float32))
    (sum_in, sum_out, sum_gain, sum_kernel), (mixed, field_grad) = lax.scan(sample_step, start, (fields, cotangent))
    factor = 1.0 / math.sqrt(CELLS)
    return (mixed, field_grad, sum_kernel * factor, sum_gain * factor, sum_in * factor, sum_out * factor)
```

```python
import functools
import math

import jax
import jax.numpy as jnp
from jax import lax
from jax.experimental import pallas as pl
from jax.experimental.pallas import tpu as pltpu
from jax.sharding import PartitionSpec as P

MESH = pl.DeviceIdType.MESH
F32 = jnp.float32
BF16 = jnp.bfloat16

eps = 1e-06
inv_root2 = 0.7071067811865476
inv_root_tau = 0.3989422804014327

TOP = 8
CONTRACT_LAST = (((1,), (1,)), ((), ()))
CONTRACT_FIRST = (((0,), (0,)), ((), ()))


def dot(lhs, rhs, dims=(((1,), (0,)), ((), ()))):
    return lax.dot_general(lhs, rhs, dims, preferred_element_type=F32)


def kernel_body(
    tiles, hi, height, width, channels, factor, n_sems,
    x_ref, seam_ref, kern_ref, gain_ref, win_ref, wout_ref, cot_ref,
    mixed_ref, fgrad_ref, kgrad_ref, ggrad_ref, wing_ref, woutg_ref,
    ext, dpad, flip, flip2, tmp, normed, rstd_ref, own_ds, own_br, hid, dpre, pre_ref, dhid_ref,
    hs, hr, adj_s, adj_r, core,
    sc_all, cot_all, ds_s, ds_r, br_s, br_r,
    gf, gs, xr, part, zs, zr, agz, agx,
    kfull, kr, kl, klr, kz, kf,
    send_sems, recv_sems,
):
    cells = height * width
    half = channels // 2
    t = lax.axis_index("tile")
    f = lax.axis_index("fsdp")
    west = lax.rem(t + tiles - 1, tiles)
    east = lax.rem(t + 1, tiles)
    x = lax.rem(t, 2)
    z = t // 2
    x_peer = z * 2 + (1 - x)
    z_at = [lax.rem(z + r, hi) for r in range(hi)]
    z_from = [lax.rem(z + hi - r, hi) for r in range(hi)]
    z_peer = [at * 2 + x for at in z_at]
    f_peer = [f, f + 1 - 2 * lax.rem(f, 2), lax.rem(f + 2, 4), 3 - f]

    barrier = pltpu.get_barrier_semaphore()
    greet = (
        [{"fsdp": f_peer[r]} for r in (1, 2, 3)]
        + [{"tile": west}, {"tile": east}, {"tile": x_peer}]
        + [{"tile": z_peer[r]} for r in range(1, hi)]
    )
    for device in greet:
        pl.semaphore_signal(barrier, inc=1, device_id=device, device_id_type=MESH)

    started = []

    def send(src, dst, device):
        index = len(started)
        copy = pltpu.make_async_remote_copy(
            src_ref=src, dst_ref=dst, send_sem=send_sems.at[index],
            recv_sem=recv_sems.at[index], device_id=device, device_id_type=MESH,
        )
        copy.start()
        started.append(copy)
        return index

    def arrived(index, ref):
        pltpu.make_async_remote_copy(
            src_ref=ref, dst_ref=ref, send_sem=send_sems.at[index],
            recv_sem=recv_sems.at[index], device_id={"tile": t, "fsdp": f}, device_id_type=MESH,
        ).wait_recv()

    def rows_of(j):
        return pl.ds(j * height, height)

    groups = [slice(128 * g, 128 * g + 128) for g in range(channels // 128)]

    def spread(ref, by_lanes):
        for g, lanes in enumerate(groups):
            by_lanes[g] = ref[:, lanes].astype(F32)

    def column_of(by_lanes, j):
        return jnp.concatenate(
            [by_lanes[g, pl.ds(j, height, stride=width), :] for g in range(len(groups))], axis=1
        )

    def put_column(by_lanes, j, value):
        for g, lanes in enumerate(groups):
            by_lanes[g, pl.ds(j, height, stride=width), :] = value[:, lanes]

    def gather_lanes(by_lanes, ref):
        for g, lanes in enumerate(groups):
            ref[:, lanes] = by_lanes[g].astype(BF16)

    spread(x_ref, flip)
    spread(cot_ref, flip2)
    for j in range(width):
        column = column_of(flip, j)
        ext[3 + j, TOP : TOP + height, :] = column
        if j < 3:
            hs[0, rows_of(j), :] = column.astype(BF16)
        if j >= width - 3:
            hs[1, rows_of(j - width + 3), :] = column.astype(BF16)
    pl.semaphore_wait(barrier, len(greet))
    halo_w = send(hs.at[0], hr.at[1], {"tile": west})
    halo_e = send(hs.at[1], hr.at[0], {"tile": east})
    for j in range(width):
        cot_all[0, rows_of(j), :] = column_of(flip2, j).astype(BF16)
    cot_id = [None] + [send(cot_all.at[0], cot_all.at[r], {"fsdp": f_peer[r]}) for r in (1, 2, 3)]
    bottom = ext.shape[1] - TOP - height
    ext[:, 0:TOP, :] = jnp.zeros((width + 6, TOP, channels), F32)
    ext[:, TOP + height :, :] = jnp.zeros((width + 6, bottom, channels), F32)
    dpad[:, 0:TOP, :] = jnp.zeros((width, TOP, channels), F32)
    dpad[:, TOP + height :, :] = jnp.zeros((width, bottom, channels), F32)

    row_at = lax.broadcasted_iota(jnp.int32, (height, height), 0)
    col_at = lax.broadcasted_iota(jnp.int32, (height, height), 1)

    def picker(offset):
        return jnp.where(col_at == row_at + offset, 1.0, 0.0).astype(BF16)

    arrived(halo_w, hr.at[1])
    arrived(halo_e, hr.at[0])
    for side, first in ((0, 0), (1, width + 3)):
        pick = picker(seam_ref[0, side])
        for j in range(3):
            ext[first + j, TOP : TOP + height, :] = dot(pick, hr[side, rows_of(j), :])

    lane_groups = channels // 128

    def lanes_of(g):
        return pl.ds(pl.multiple_of(g * 128, 128), 128)

    @pl.loop(0, lane_groups)
    def _(g):
        lanes = lanes_of(g)
        total = jnp.zeros((width, height, 128), F32)
        for a in range(7):
            shifted = ext[:, TOP - 3 + a : TOP - 3 + a + height, lanes]
            for b in range(7):
                total = total + shifted[b : b + width] * kern_ref[pl.ds(7 * a + b, 1), lanes][None]
        tmp[:, lanes] = total.reshape(cells, 128)

    gain = gain_ref[...]

    @pl.loop(0, width)
    def _(j):
        at = pl.ds(pl.multiple_of(j * height, height), height)
        rows = tmp[at, :]
        centered = rows - jnp.mean(rows, axis=-1, keepdims=True)
        rstd = lax.rsqrt(jnp.mean(centered * centered, axis=-1, keepdims=True) + eps)
        unit = centered * rstd
        normed[at, :] = unit
        rstd_ref[at, :] = jnp.broadcast_to(rstd, (height, 128))
        sc_all[0, at, :] = (unit * gain).astype(BF16)

    sc_id = [None] + [send(sc_all.at[0], sc_all.at[r], {"fsdp": f_peer[r]}) for r in (1, 2, 3)]

    w_in = win_ref[...]
    w_out = wout_ref[...]
    ds_id = [None] * 4
    for r in range(4):
        if r > 0:
            arrived(cot_id[r], cot_all.at[r])
        dhid_ref[...] = dot(cot_all[r], w_out, CONTRACT_LAST)
        if r > 0:
            arrived(sc_id[r], sc_all.at[r])
        pre_ref[...] = dot(sc_all[r], w_in)

        @pl.loop(0, width)
        def _(j):
            at = pl.ds(pl.multiple_of(j * height, height), height)
            pre = pre_ref[at, :]
            phi = 0.5 * (1.0 + lax.erf(pre * inv_root2))
            slope = phi + pre * inv_root_tau * jnp.exp(-0.5 * pre * pre)
            hid[r, at, :] = (pre * phi).astype(BF16)
            dpre[r, at, :] = (dhid_ref[at, :] * slope).astype(BF16)

        back = dot(dpre[r], w_in, CONTRACT_LAST)
        if r == 0:
            own_ds[...] = back
        else:
            ds_s[r - 1] = back.astype(BF16)
            ds_id[r] = send(ds_s.at[r - 1], ds_r.at[r - 1], {"fsdp": f_peer[r]})

    def term_start(h, lhs, rhs):
        total = dot(lhs[0], rhs[0], CONTRACT_FIRST)
        for r in range(1, 4):
            total = total + dot(lhs[r], rhs[r], CONTRACT_FIRST)
        for side in range(2):
            gf[h, side] = total[:, side * half : (side + 1) * half]
            gs[h, side] = total[:, side * half : (side + 1) * half].astype(BF16)
        return send(gs.at[h, 1 - x], xr.at[h], {"tile": x_peer})

    piece = channels // hi

    def term_mid(h, index):
        arrived(index, xr.at[h])
        part[h] = gf[h, x] + xr[h].astype(F32)
        for r in range(hi):
            zs[h, r] = part[h, pl.ds(pl.multiple_of(z_at[r] * piece, piece), piece), :].astype(BF16)
        return [None] + [
            send(zs.at[h, r], zr.at[h, r], {"tile": z_peer[r]}) for r in range(1, hi)
        ]

    def term_sum(h, ids):
        total = part[h, pl.ds(pl.multiple_of(z * piece, piece), piece), :]
        for r in range(1, hi):
            arrived(ids[r], zr.at[h, r])
            total = total + zr[h, r].astype(F32)
        agz[h, z] = (total * factor).astype(BF16)
        return [None] + [
            send(agz.at[h, z], agz.at[h, z], {"tile": z_peer[r]}) for r in range(1, hi)
        ]

    def term_spread(h, ids):
        for r in range(1, hi):
            arrived(ids[r], agz.at[h, z_from[r]])
        return send(agz.at[h], agx.at[h], {"tile": x_peer})

    def lanes_half(side):
        return pl.ds(pl.multiple_of(side * half, half), half)

    def term_end(h, index, out_ref):
        out_ref[:, lanes_half(x)] = agz[h].astype(F32).reshape(channels, half)
        arrived(index, agx.at[h])
        out_ref[:, lanes_half(1 - x)] = agx[h].astype(F32).reshape(channels, half)

    x_ids = [term_start(0, hid, cot_all), term_start(1, sc_all, dpre)]

    br_id = [None] * 4
    for r in (1, 2, 3, 0):
        branch = dot(hid[r], w_out)
        if r == 0:
            own_br[...] = branch
        else:
            br_s[r - 1] = branch.astype(BF16)
            br_id[r] = send(br_s.at[r - 1], br_r.at[r - 1], {"fsdp": f_peer[r]})

    for r in (1, 2, 3):
        arrived(ds_id[r], ds_r.at[r - 1])

    def norm_back(j, term_gain):
        at = pl.ds(pl.multiple_of(j * height, height), height)
        d_scaled = own_ds[at, :]
        for r in range(3):
            d_scaled = d_scaled + ds_r[r, at, :].astype(F32)
        unit = normed[at, :]
        both = d_scaled * unit
        g = d_scaled * gain
        mean_g = jnp.mean(g, axis=-1, keepdims=True)
        mean_gn = jnp.mean(g * unit, axis=-1, keepdims=True)
        dpad[j, TOP : TOP + height, :] = (g - mean_g - unit * mean_gn) * rstd_ref[at, 0:1]
        return term_gain + jnp.sum(both.reshape(height // 8, 8, channels), axis=0)

    term_gain = lax.fori_loop(0, width, norm_back, jnp.zeros((8, channels), F32))
    z_ids = [term_mid(0, x_ids[0]), None]

    kfull[3] = jnp.zeros((16, channels), F32)
    kfull[3, 1:2, :] = jnp.sum(term_gain, axis=0, keepdims=True)

    @pl.loop(0, lane_groups)
    def _(g):
        lanes = lanes_of(g)
        d_here = dpad[:, TOP : TOP + height, lanes]
        for a in range(7):
            shifted = ext[:, TOP - 3 + a : TOP - 3 + a + height, lanes]
            for b in range(7):
                tap = 7 * a + b
                both = (d_here * shifted[b : b + width]).reshape(cells // 8, 8, 128)
                column = jnp.sum(jnp.sum(both, axis=0), axis=0, keepdims=True)
                kfull[tap // 16, tap % 16 : tap % 16 + 1, lanes] = column

    kr_id = [None] + [
        send(kfull.at[f_peer[r]], kr.at[r - 1], {"fsdp": f_peer[r]}) for r in (1, 2, 3)
    ]
    z_ids[1] = term_mid(1, x_ids[1])

    @pl.loop(0, lane_groups)
    def _(g):
        lanes = lanes_of(g)
        total = [jnp.zeros((height, 128), F32) for _ in range(width + 6)]
        for a in range(7):
            first = TOP + 3 - a
            shifted = dpad[:, first : first + height, lanes]
            for b in range(7):
                tap = kern_ref[pl.ds(7 * a + b, 1), lanes]
                for j in range(width):
                    total[j + b] = total[j + b] + shifted[j] * tap
        for j in range(width + 6):
            core[j, :, lanes] = total[j]

    for side, first in ((0, 0), (1, width + 3)):
        pick = picker(-seam_ref[0, side])
        for j in range(3):
            adj_s[side, rows_of(j), :] = dot(pick, core[first + j].astype(BF16)).astype(BF16)
    adj_w = send(adj_s.at[0], adj_r.at[1], {"tile": west})
    adj_e = send(adj_s.at[1], adj_r.at[0], {"tile": east})

    total = kfull[f]
    for r in (1, 2, 3):
        arrived(kr_id[r], kr.at[r - 1])
        total = total + kr[r - 1]
    kl[...] = total
    kl_id = send(kl, klr, {"tile": x_peer})

    g_ids = [term_sum(0, z_ids[0]), None]

    arrived(kl_id, klr)
    kz[z] = kl[...] + klr[...]
    kz_id = [None] + [send(kz.at[z], kz.at[z], {"tile": z_peer[r]}) for r in range(1, hi)]

    g_ids[1] = term_sum(1, z_ids[1])

    for r in (1, 2, 3):
        arrived(br_id[r], br_r.at[r - 1])
    for j in range(width):
        at = rows_of(j)
        value = ext[3 + j, TOP : TOP + height, :] + own_br[at, :]
        for r in range(3):
            value = value + br_r[r, at, :].astype(F32)
        put_column(flip2, j, value)
    gather_lanes(flip2, mixed_ref)

    for r in range(1, hi):
        arrived(kz_id[r], kz.at[z_from[r]])
    total = kz[0]
    for at in range(1, hi):
        total = total + kz[at]
    kf[f] = total * factor
    kf_id = [None] + [send(kf.at[f], kf.at[f], {"fsdp": f_peer[r]}) for r in (1, 2, 3)]

    last = [term_spread(0, g_ids[0]), None]

    arrived(adj_w, adj_r.at[1])
    arrived(adj_e, adj_r.at[0])
    for j in range(width):
        value = cot_all[0, rows_of(j), :].astype(F32) + core[3 + j]
        if j < 3:
            value = value + adj_r[0, rows_of(j), :].astype(F32)
        if j >= width - 3:
            value = value + adj_r[1, rows_of(j - width + 3), :].astype(F32)
        put_column(flip, j, value)
    gather_lanes(flip, fgrad_ref)

    last[1] = term_spread(1, g_ids[1])

    for r in (1, 2, 3):
        arrived(kf_id[r], kf.at[f_peer[r]])
    for at in range(3):
        kgrad_ref[16 * at : 16 * at + 16, :] = kf[at]
    kgrad_ref[48:49, :] = kf[3, 0:1, :]
    ggrad_ref[...] = kf[3, 1:2, :]

    term_end(0, last[0], woutg_ref)
    term_end(1, last[1], wing_ref)
    for copy in started:
        copy.wait_send()
    if len(started) != n_sems:
        raise ValueError(len(started))


def body(tiles, shards, fields, seam_shift, kernel, gain, w_in, w_out, cotangent):
    _, height, width, channels = fields.shape
    cells = height * width
    hidden = w_in.shape[1]
    assert shards == 4 and tiles % 2 == 0 and kernel.shape[0] == 49
    assert hidden == channels and channels % (16 * (tiles // 2)) == 0
    hi = tiles // 2
    factor = 1.0 / math.sqrt(cells * tiles * shards)
    half = channels // 2
    piece = channels // hi
    n_sems = 2 + 3 + 3 + 3 + 3 + 2 + 2 * (2 + 2 * (hi - 1)) + 3 + 1 + (hi - 1) + 3
    padded = height + 16

    def vmem(shape, kind):
        return pltpu.VMEM(shape, kind)

    whole = pl.BlockSpec(memory_space=pltpu.VMEM)
    rows = (cells, channels)
    outs = pl.pallas_call(
        functools.partial(kernel_body, tiles, hi, height, width, channels, factor, n_sems),
        out_shape=(
            jax.ShapeDtypeStruct(rows, BF16),
            jax.ShapeDtypeStruct(rows, BF16),
            jax.ShapeDtypeStruct(kernel.shape, F32),
            jax.ShapeDtypeStruct((1, channels), F32),
            jax.ShapeDtypeStruct(w_in.shape, F32),
            jax.ShapeDtypeStruct(w_out.shape, F32),
        ),
        in_specs=[
            whole, pl.BlockSpec(memory_space=pltpu.SMEM), whole, whole, whole, whole, whole,
        ],
        out_specs=[whole] * 6,
        scratch_shapes=[
            vmem((width + 6, padded, channels), F32),
            vmem((width, padded, channels), F32),
            vmem((channels // 128, cells, 128), F32),
            vmem((channels // 128, cells, 128), F32),
            vmem(rows, F32),
            vmem(rows, F32),
            vmem((cells, 128), F32),
            vmem(rows, F32),
            vmem(rows, F32),
            vmem((4, cells, hidden), BF16),
            vmem((4, cells, hidden), BF16),
            vmem((cells, hidden), F32),
            vmem((cells, hidden), F32),
            vmem((2, 3 * height, channels), BF16),
            vmem((2, 3 * height, channels), BF16),
            vmem((2, 3 * height, channels), BF16),
            vmem((2, 3 * height, channels), BF16),
            vmem((width + 6, height, channels), F32),
            vmem((4, cells, channels), BF16),
            vmem((4, cells, channels), BF16),
            vmem((3, cells, channels), BF16),
            vmem((3, cells, channels), BF16),
            vmem((3, cells, channels), BF16),
            vmem((3, cells, channels), BF16),
            vmem((2, 2, channels, half), F32),
            vmem((2, 2, channels, half), BF16),
            vmem((2, channels, half), BF16),
            vmem((2, channels, half), F32),
            vmem((2, hi, piece, half), BF16),
            vmem((2, hi, piece, half), BF16),
            vmem((2, hi, piece, half), BF16),
            vmem((2, hi, piece, half), BF16),
            vmem((4, 16, channels), F32),
            vmem((3, 16, channels), F32),
            vmem((16, channels), F32),
            vmem((16, channels), F32),
            vmem((hi, 16, channels), F32),
            vmem((4, 16, channels), F32),
            pltpu.SemaphoreType.DMA((n_sems,)),
            pltpu.SemaphoreType.DMA((n_sems,)),
        ],
        compiler_params=pltpu.CompilerParams(
            collective_id=0, has_side_effects=True, vmem_limit_bytes=48 * 1024 * 1024
        ),
        name="block",
    )(
        fields.reshape(rows), seam_shift, kernel, gain.reshape(1, channels), w_in, w_out,
        cotangent.reshape(rows),
    )
    mixed, field_grad, kernel_grad, gain_grad, w_in_grad, w_out_grad = outs
    return (
        mixed.reshape(fields.shape), field_grad.reshape(fields.shape), kernel_grad,
        gain_grad.reshape(channels), w_in_grad, w_out_grad,
    )


def solution(mesh):
    return jax.shard_map(
        functools.partial(body, mesh.shape["tile"], mesh.shape["fsdp"]),
        mesh=mesh,
        in_specs=(
            P("fsdp", None, "tile", None),
            P("tile", None),
            P(),
            P(),
            P(None, "fsdp"),
            P("fsdp", None),
            P("fsdp", None, "tile", None),
        ),
        out_specs=(
            P("fsdp", None, "tile", None),
            P("fsdp", None, "tile", None),
            P(),
            P(),
            P(None, "fsdp"),
            P("fsdp", None),
        ),
        check_vma=False,
    )
```

```python
import functools
import math

import jax
import jax.numpy as jnp
from jax import lax
from jax.experimental import pallas as pl
from jax.experimental.pallas import tpu as pltpu
from jax.sharding import PartitionSpec as P

MESH = pl.DeviceIdType.MESH
F32 = jnp.float32
BF16 = jnp.bfloat16

eps = 1e-06
inv_root2 = 0.7071067811865476
inv_root_tau = 0.3989422804014327

TOP = 8
CONTRACT_LAST = (((1,), (1,)), ((), ()))
CONTRACT_FIRST = (((0,), (0,)), ((), ()))


def dot(lhs, rhs, dims=(((1,), (0,)), ((), ()))):
    return lax.dot_general(lhs, rhs, dims, preferred_element_type=F32)


def kernel_body(
    tiles, hi, height, width, channels, factor, n_sems,
    x_hbm, seam_ref, kern_hbm, gain_hbm, win_hbm, wout_hbm, cot_hbm,
    mixed_hbm, fgrad_hbm, kgrad_hbm, ggrad_hbm, wing_hbm, woutg_hbm,
    ext, dpad, flip, flip2, tmp, normed, rstd_ref, own_ds, keep_ds, own_br, keep_br, hid, dpre, pre_ref, dhid_ref,
    hs, hr, adj_s, adj_r, core,
    sc_all, cot_all, ds_s, ds_r, br_s, br_r,
    gf, gs, xr, part, zs, zr, agz, agx,
    kfull, kr, kl, klr, kz, kf,
    x_ref, kern_ref, gain_ref, win_ref, wout_ref, cot_ref,
    mixed_ref, fgrad_ref, kgrad_ref, ggrad_ref, wing_ref, woutg_ref,
    load_sems, store_sems, send_sems, recv_sems,
):
    pairs = (
        (x_hbm, x_ref), (cot_hbm, cot_ref), (kern_hbm, kern_ref), (gain_hbm, gain_ref),
        (wout_hbm, wout_ref), (win_hbm, win_ref),
    )
    loads = [
        pltpu.make_async_copy(src, dst, load_sems.at[i]) for i, (src, dst) in enumerate(pairs)
    ]
    for load in loads:
        load.start()
    stores = []

    def store(src, dst):
        stores.append(pltpu.make_async_copy(src, dst, store_sems.at[len(stores)]))
        stores[-1].start()

    cells = height * width
    half = channels // 4
    t = lax.axis_index("tile")
    f = lax.axis_index("fsdp")
    west = lax.rem(t + tiles - 1, tiles)
    east = lax.rem(t + 1, tiles)
    x = lax.rem(t, 2)
    z = t // 2
    x_peer = z * 2 + (1 - x)
    z_at = [lax.rem(z + r, hi) for r in range(hi)]
    z_from = [lax.rem(z + hi - r, hi) for r in range(hi)]
    z_peer = [at * 2 + x for at in z_at]
    f_peer = [f, f + 1 - 2 * lax.rem(f, 2), lax.rem(f + 2, 4), 3 - f]

    barrier = pltpu.get_barrier_semaphore()
    greet = (
        [{"fsdp": f_peer[r]} for r in (1, 2, 3)]
        + [{"tile": west}, {"tile": east}, {"tile": x_peer}]
        + [{"tile": z_peer[r]} for r in range(1, hi)]
    )
    for device in greet:
        pl.semaphore_signal(barrier, inc=1, device_id=device, device_id_type=MESH)

    started = []

    def send(src, dst, device):
        index = len(started)
        copy = pltpu.make_async_remote_copy(
            src_ref=src, dst_ref=dst, send_sem=send_sems.at[index],
            recv_sem=recv_sems.at[index], device_id=device, device_id_type=MESH,
        )
        copy.start()
        started.append(copy)
        return index

    def arrived(index, ref):
        pltpu.make_async_remote_copy(
            src_ref=ref, dst_ref=ref, send_sem=send_sems.at[index],
            recv_sem=recv_sems.at[index], device_id={"tile": t, "fsdp": f}, device_id_type=MESH,
        ).wait_recv()

    def rows_of(j):
        return pl.ds(j * height, height)

    groups = [slice(128 * g, 128 * g + 128) for g in range(channels // 128)]

    def spread(ref, by_lanes):
        for g, lanes in enumerate(groups):
            by_lanes[g] = ref[:, lanes].astype(F32)

    def column_of(by_lanes, j):
        return jnp.concatenate(
            [by_lanes[g, pl.ds(j, height, stride=width), :] for g in range(len(groups))], axis=1
        )

    def put_column(by_lanes, j, value):
        for g, lanes in enumerate(groups):
            by_lanes[g, pl.ds(j, height, stride=width), :] = value[:, lanes]

    def gather_lanes(by_lanes, ref):
        for g, lanes in enumerate(groups):
            ref[:, lanes] = by_lanes[g].astype(BF16)

    loads[0].wait()
    spread(x_ref, flip)
    for j in range(width):
        column = column_of(flip, j)
        ext[3 + j, TOP : TOP + height, :] = column
        if j < 3:
            hs[0, rows_of(j), :] = column.astype(BF16)
        if j >= width - 3:
            hs[1, rows_of(j - width + 3), :] = column.astype(BF16)
    pl.semaphore_wait(barrier, len(greet))
    halo_w = send(hs.at[0], hr.at[1], {"tile": west})
    halo_e = send(hs.at[1], hr.at[0], {"tile": east})
    loads[1].wait()
    spread(cot_ref, flip2)
    for j in range(width):
        cot_all[0, rows_of(j), :] = column_of(flip2, j).astype(BF16)
    sibling = {"fsdp": f_peer[1]}
    across = {"fsdp": f_peer[2]}
    cot_id = [
        None,
        send(cot_all.at[0], cot_all.at[1], sibling),
        send(cot_all.at[0], cot_all.at[2], across),
        None,
    ]
    bottom = ext.shape[1] - TOP - height
    ext[:, 0:TOP, :] = jnp.zeros((width + 6, TOP, channels), F32)
    ext[:, TOP + height :, :] = jnp.zeros((width + 6, bottom, channels), F32)
    dpad[:, 0:TOP, :] = jnp.zeros((width, TOP, channels), F32)
    dpad[:, TOP + height :, :] = jnp.zeros((width, bottom, channels), F32)

    row_at = lax.broadcasted_iota(jnp.int32, (height, height), 0)
    col_at = lax.broadcasted_iota(jnp.int32, (height, height), 1)

    def picker(offset):
        return jnp.where(col_at == row_at + offset, 1.0, 0.0).astype(BF16)

    def lanes_of(g):
        return pl.ds(pl.multiple_of(g * 128, 128), 128)

    def conv_part(columns, fresh):
        @pl.loop(0, channels // 128)
        def _(g):
            lanes = lanes_of(g)
            total = [
                jnp.zeros((height, 128), F32) if fresh else tmp[rows_of(j), lanes]
                for j in range(width)
            ]
            for a in range(7):
                first = TOP - 3 + a
                shifted = {c: ext[c, first : first + height, lanes] for c in columns}
                for b in range(7):
                    tap = kern_ref[pl.ds(7 * a + b, 1), lanes]
                    for j in range(width):
                        if j + b in shifted:
                            total[j] = total[j] + shifted[j + b] * tap
            for j in range(width):
                tmp[rows_of(j), lanes] = total[j]

    loads[2].wait()
    conv_part(list(range(3, width + 3)), True)
    arrived(halo_w, hr.at[1])
    arrived(halo_e, hr.at[0])
    for side, first in ((0, 0), (1, width + 3)):
        pick = picker(seam_ref[0, side])
        for j in range(3):
            ext[first + j, TOP : TOP + height, :] = dot(pick, hr[side, rows_of(j), :])
    conv_part([0, 1, 2, width + 3, width + 4, width + 5], False)

    loads[3].wait()
    gain = gain_ref[...]

    @pl.loop(0, width)
    def _(j):
        at = pl.ds(pl.multiple_of(j * height, height), height)
        rows = tmp[at, :]
        centered = rows - jnp.mean(rows, axis=-1, keepdims=True)
        rstd = lax.rsqrt(jnp.mean(centered * centered, axis=-1, keepdims=True) + eps)
        unit = centered * rstd
        normed[at, :] = unit
        rstd_ref[at, :] = jnp.broadcast_to(rstd, (height, 128))
        sc_all[0, at, :] = (unit * gain).astype(BF16)

    sc_id = [
        None,
        send(sc_all.at[0], sc_all.at[1], sibling),
        send(sc_all.at[0], sc_all.at[2], across),
        None,
    ]
    loads[4].wait()
    loads[5].wait()
    w_in = win_ref[...]
    w_out = wout_ref[...]
    ds_id = [None] * 4
    for r in range(4):
        if r > 0:
            arrived(cot_id[r], cot_all.at[r])
        if r == 2:
            cot_id[3] = send(cot_all.at[2], cot_all.at[3], sibling)
        dhid_ref[...] = dot(cot_all[r], w_out, CONTRACT_LAST)
        if r > 0:
            arrived(sc_id[r], sc_all.at[r])
        if r == 2:
            sc_id[3] = send(sc_all.at[2], sc_all.at[3], sibling)
        pre_ref[...] = dot(sc_all[r], w_in)

        @pl.loop(0, width)
        def _(j):
            at = pl.ds(pl.multiple_of(j * height, height), height)
            pre = pre_ref[at, :]
            phi = 0.5 * (1.0 + lax.erf(pre * inv_root2))
            slope = phi + pre * inv_root_tau * jnp.exp(-0.5 * pre * pre)
            hid[r, at, :] = (pre * phi).astype(BF16)
            dpre[r, at, :] = (dhid_ref[at, :] * slope).astype(BF16)

        back = dot(dpre[r], w_in, CONTRACT_LAST)
        if r == 0:
            own_ds[...] = back
        elif r == 2:
            keep_ds[...] = back
        else:
            slot = r // 2
            ds_s[slot] = back.astype(BF16)
            ds_id[r] = send(ds_s.at[slot], ds_r.at[slot], sibling)

    def term_start(h):
        lhs, rhs = ((hid, cot_all), (sc_all, dpre))[h // 2]
        lanes = slice((h % 2) * 2 * half, (h % 2) * 2 * half + 2 * half)
        total = dot(lhs[0], rhs[0, :, lanes], CONTRACT_FIRST)
        for r in range(1, 4):
            total = total + dot(lhs[r], rhs[r, :, lanes], CONTRACT_FIRST)
        for side in range(2):
            gf[h, side] = total[:, side * half : (side + 1) * half]
            gs[h, side] = total[:, side * half : (side + 1) * half].astype(BF16)
        return send(gs.at[h, 1 - x], xr.at[h], {"tile": x_peer})

    piece = channels // hi

    def term_mid(h, index):
        arrived(index, xr.at[h])
        part[h] = gf[h, x] + xr[h].astype(F32)
        for r in range(1, hi):
            zs[h, r] = part[h, pl.ds(pl.multiple_of(z_at[r] * piece, piece), piece), :].astype(BF16)
        return [None] + [
            send(zs.at[h, r], zr.at[h, r], {"tile": z_peer[r]}) for r in range(1, hi)
        ]

    def term_sum(h, ids):
        total = part[h, pl.ds(pl.multiple_of(z * piece, piece), piece), :]
        for r in range(1, hi):
            arrived(ids[r], zr.at[h, r])
            total = total + zr[h, r].astype(F32)
        agz[h, z] = (total * factor).astype(BF16)
        return [None] + [
            send(agz.at[h, z], agz.at[h, z], {"tile": z_peer[r]}) for r in range(1, hi)
        ]

    def term_spread(h, ids):
        for r in range(1, hi):
            arrived(ids[r], agz.at[h, z_from[r]])
        return send(agz.at[h], agx.at[h], {"tile": x_peer})

    def term_put(h, side, value):
        ref = (woutg_ref, wing_ref)[h // 2]
        lanes = pl.ds(pl.multiple_of(((h % 2) * 2 + side) * half, half), half)
        ref[:, lanes] = value.astype(F32).reshape(channels, half)

    def term_end(h, index):
        arrived(index, agx.at[h])
        term_put(h, 1 - x, agx[h])

    x_ids, z_ids, g_ids, last = [None] * 4, [None] * 4, [None] * 4, [None] * 4
    x_ids[0] = term_start(0)

    arrived(ds_id[3], ds_r.at[1])
    ds_s[2] = (keep_ds[...] + ds_r[1].astype(F32)).astype(BF16)
    ds_id[2] = send(ds_s.at[2], ds_r.at[2], across)

    for h in (1, 2, 3):
        x_ids[h] = term_start(h)

    br_id = [None] * 4
    for r in (3, 1, 2, 0):
        branch = dot(hid[r], w_out)
        if r == 0:
            own_br[...] = branch
        elif r == 2:
            keep_br[...] = branch
        else:
            slot = r // 2
            br_s[slot] = branch.astype(BF16)
            br_id[r] = send(br_s.at[slot], br_r.at[slot], sibling)

    z_ids[0] = term_mid(0, x_ids[0])
    z_ids[1] = term_mid(1, x_ids[1])
    arrived(ds_id[1], ds_r.at[0])
    arrived(ds_id[2], ds_r.at[2])

    def norm_back(j, term_gain):
        at = pl.ds(pl.multiple_of(j * height, height), height)
        d_scaled = own_ds[at, :]
        for r in (0, 2):
            d_scaled = d_scaled + ds_r[r, at, :].astype(F32)
        unit = normed[at, :]
        both = d_scaled * unit
        g = d_scaled * gain
        mean_g = jnp.mean(g, axis=-1, keepdims=True)
        mean_gn = jnp.mean(g * unit, axis=-1, keepdims=True)
        dpad[j, TOP : TOP + height, :] = (g - mean_g - unit * mean_gn) * rstd_ref[at, 0:1]
        return term_gain + jnp.sum(both.reshape(height // 8, 8, channels), axis=0)

    term_gain = lax.fori_loop(0, width, norm_back, jnp.zeros((8, channels), F32))
    z_ids[2] = term_mid(2, x_ids[2])

    def adjoint(columns):
        @pl.loop(0, channels // 128)
        def _(g):
            lanes = lanes_of(g)
            total = {c: jnp.zeros((height, 128), F32) for c in columns}
            for a in range(7):
                first = TOP + 3 - a
                shifted = [dpad[j, first : first + height, lanes] for j in range(width)]
                for b in range(7):
                    tap = kern_ref[pl.ds(7 * a + b, 1), lanes]
                    for j in range(width):
                        if j + b in total:
                            total[j + b] = total[j + b] + shifted[j] * tap
            for c in columns:
                core[c, :, lanes] = total[c]

    adjoint([0, 1, 2, width + 3, width + 4, width + 5])
    for side, first in ((0, 0), (1, width + 3)):
        pick = picker(-seam_ref[0, side])
        for j in range(3):
            adj_s[side, rows_of(j), :] = dot(pick, core[first + j].astype(BF16)).astype(BF16)
    adj_w = send(adj_s.at[0], adj_r.at[1], {"tile": west})
    adj_e = send(adj_s.at[1], adj_r.at[0], {"tile": east})
    z_ids[3] = term_mid(3, x_ids[3])

    kfull[3] = jnp.zeros((16, channels), F32)
    kfull[3, 1:2, :] = jnp.sum(term_gain, axis=0, keepdims=True)

    @pl.loop(0, channels // 128)
    def _(g):
        lanes = lanes_of(g)
        d_here = dpad[:, TOP : TOP + height, lanes]
        for a in range(7):
            shifted = ext[:, TOP - 3 + a : TOP - 3 + a + height, lanes]
            for b in range(7):
                tap = 7 * a + b
                both = (d_here * shifted[b : b + width]).reshape(cells // 8, 8, 128)
                column = jnp.sum(jnp.sum(both, axis=0), axis=0, keepdims=True)
                kfull[tap // 16, tap % 16 : tap % 16 + 1, lanes] = column

    kr_id = [None] + [
        send(kfull.at[f_peer[r]], kr.at[r - 1], {"fsdp": f_peer[r]}) for r in (1, 2, 3)
    ]
    g_ids[0] = term_sum(0, z_ids[0])
    g_ids[1] = term_sum(1, z_ids[1])

    arrived(br_id[3], br_r.at[1])
    br_s[2] = (keep_br[...] + br_r[1].astype(F32)).astype(BF16)
    br_id[2] = send(br_s.at[2], br_r.at[2], across)

    total = kfull[f]
    for r in (1, 2, 3):
        arrived(kr_id[r], kr.at[r - 1])
        total = total + kr[r - 1]
    kl[...] = total
    kl_id = send(kl, klr, {"tile": x_peer})
    g_ids[2] = term_sum(2, z_ids[2])

    adjoint(list(range(3, width + 3)))

    arrived(kl_id, klr)
    kz[z] = kl[...] + klr[...]
    kz_id = [None] + [send(kz.at[z], kz.at[z], {"tile": z_peer[r]}) for r in range(1, hi)]
    g_ids[3] = term_sum(3, z_ids[3])
    last[0] = term_spread(0, g_ids[0])
    last[1] = term_spread(1, g_ids[1])

    arrived(adj_w, adj_r.at[1])
    arrived(adj_e, adj_r.at[0])
    for j in range(width):
        value = cot_all[0, rows_of(j), :].astype(F32) + core[3 + j]
        if j < 3:
            value = value + adj_r[0, rows_of(j), :].astype(F32)
        if j >= width - 3:
            value = value + adj_r[1, rows_of(j - width + 3), :].astype(F32)
        put_column(flip, j, value)
    gather_lanes(flip, fgrad_ref)
    store(fgrad_ref, fgrad_hbm)

    for r in range(1, hi):
        arrived(kz_id[r], kz.at[z_from[r]])
    total = kz[0]
    for at in range(1, hi):
        total = total + kz[at]
    kf[f] = total * factor
    kf_id = [None] + [send(kf.at[f], kf.at[f], {"fsdp": f_peer[r]}) for r in (1, 2, 3)]

    last[2] = term_spread(2, g_ids[2])

    arrived(br_id[1], br_r.at[0])
    arrived(br_id[2], br_r.at[2])
    for j in range(width):
        at = rows_of(j)
        value = ext[3 + j, TOP : TOP + height, :] + own_br[at, :]
        for r in (0, 2):
            value = value + br_r[r, at, :].astype(F32)
        put_column(flip2, j, value)
    gather_lanes(flip2, mixed_ref)
    store(mixed_ref, mixed_hbm)

    last[3] = term_spread(3, g_ids[3])

    for r in (1, 2, 3):
        arrived(kf_id[r], kf.at[f_peer[r]])
    for at in range(3):
        kgrad_ref[16 * at : 16 * at + 16, :] = kf[at]
    kgrad_ref[48:49, :] = kf[3, 0:1, :]
    ggrad_ref[...] = kf[3, 1:2, :]
    store(kgrad_ref, kgrad_hbm)
    store(ggrad_ref, ggrad_hbm)

    for h in range(4):
        term_put(h, x, agz[h])
    for h in range(4):
        term_end(h, last[h])
        if h == 1:
            store(woutg_ref, woutg_hbm)
    store(wing_ref, wing_hbm)
    for copy in stores:
        copy.wait()
    for copy in started:
        copy.wait_send()
    assert len(started) <= n_sems


def write_out(*refs):
    count = len(refs) // 2
    sems = refs[-1]
    copies = [
        pltpu.make_async_copy(refs[i], refs[count + i], sems.at[i]) for i in range(count)
    ]
    for copy in copies:
        copy.start()
    for copy in copies:
        copy.wait()


def body(tiles, shards, fields, seam_shift, kernel, gain, w_in, w_out, cotangent):
    _, height, width, channels = fields.shape
    cells = height * width
    hidden = w_in.shape[1]
    assert shards == 4 and tiles % 2 == 0 and kernel.shape[0] == 49
    assert hidden == channels and channels % (16 * (tiles // 2)) == 0
    hi = tiles // 2
    factor = 1.0 / math.sqrt(cells * tiles * shards)
    half = channels // 4
    piece = channels // hi
    n_sems = 32 + 4 * (2 + 2 * (hi - 1)) + hi
    padded = height + 16

    def vmem(shape, kind):
        return pltpu.VMEM(shape, kind)

    away = pl.BlockSpec(memory_space=pltpu.HBM)
    rows = (cells, channels)
    outs = pl.pallas_call(
        functools.partial(kernel_body, tiles, hi, height, width, channels, factor, n_sems),
        out_shape=(
            jax.ShapeDtypeStruct(rows, BF16),
            jax.ShapeDtypeStruct(rows, BF16),
            jax.ShapeDtypeStruct(kernel.shape, F32),
            jax.ShapeDtypeStruct((1, channels), F32),
            jax.ShapeDtypeStruct(w_in.shape, F32),
            jax.ShapeDtypeStruct(w_out.shape, F32),
        ),
        in_specs=[
            away, pl.BlockSpec(memory_space=pltpu.SMEM), away, away, away, away, away,
        ],
        out_specs=[away] * 6,
        scratch_shapes=[
            vmem((width + 6, padded, channels), F32),
            vmem((width, padded, channels), F32),
            vmem((channels // 128, cells, 128), F32),
            vmem((channels // 128, cells, 128), F32),
            vmem(rows, F32),
            vmem(rows, F32),
            vmem((cells, 128), F32),
            vmem(rows, F32),
            vmem(rows, F32),
            vmem(rows, F32),
            vmem(rows, F32),
            vmem((4, cells, hidden), BF16),
            vmem((4, cells, hidden), BF16),
            vmem((cells, hidden), F32),
            vmem((cells, hidden), F32),
            vmem((2, 3 * height, channels), BF16),
            vmem((2, 3 * height, channels), BF16),
            vmem((2, 3 * height, channels), BF16),
            vmem((2, 3 * height, channels), BF16),
            vmem((width + 6, height, channels), F32),
            vmem((4, cells, channels), BF16),
            vmem((4, cells, channels), BF16),
            vmem((3, cells, channels), BF16),
            vmem((3, cells, channels), BF16),
            vmem((3, cells, channels), BF16),
            vmem((3, cells, channels), BF16),
            vmem((4, 2, channels, half), F32),
            vmem((4, 2, channels, half), BF16),
            vmem((4, channels, half), BF16),
            vmem((4, channels, half), F32),
            vmem((4, hi, piece, half), BF16),
            vmem((4, hi, piece, half), BF16),
            vmem((4, hi, piece, half), BF16),
            vmem((4, hi, piece, half), BF16),
            vmem((4, 16, channels), F32),
            vmem((3, 16, channels), F32),
            vmem((16, channels), F32),
            vmem((16, channels), F32),
            vmem((hi, 16, channels), F32),
            vmem((4, 16, channels), F32),
            vmem(rows, BF16),
            vmem(kernel.shape, F32),
            vmem((1, channels), F32),
            vmem(w_in.shape, BF16),
            vmem(w_out.shape, BF16),
            vmem(rows, BF16),
            vmem(rows, BF16),
            vmem(rows, BF16),
            vmem(kernel.shape, F32),
            vmem((1, channels), F32),
            vmem(w_in.shape, F32),
            vmem(w_out.shape, F32),
            pltpu.SemaphoreType.DMA((6,)),
            pltpu.SemaphoreType.DMA((6,)),
            pltpu.SemaphoreType.DMA((n_sems,)),
            pltpu.SemaphoreType.DMA((n_sems,)),
        ],
        compiler_params=pltpu.CompilerParams(
            collective_id=0, has_side_effects=True, vmem_limit_bytes=58 * 1024 * 1024
        ),
        name="block",
    )(
        fields.reshape(rows), seam_shift, kernel, gain.reshape(1, channels), w_in, w_out,
        cotangent.reshape(rows),
    )
    outs = pl.pallas_call(
        write_out,
        out_shape=[jax.ShapeDtypeStruct(out.shape, out.dtype) for out in outs],
        in_specs=[away] * 6,
        out_specs=[away] * 6,
        scratch_shapes=[pltpu.SemaphoreType.DMA((6,))],
        compiler_params=pltpu.CompilerParams(vmem_limit_bytes=58 * 1024 * 1024),
        name="write_out",
    )(*outs)
    mixed, field_grad, kernel_grad, gain_grad, w_in_grad, w_out_grad = outs
    return (
        mixed.reshape(fields.shape), field_grad.reshape(fields.shape), kernel_grad,
        gain_grad.reshape(channels), w_in_grad, w_out_grad,
    )


def solution(mesh):
    return jax.shard_map(
        functools.partial(body, mesh.shape["tile"], mesh.shape["fsdp"]),
        mesh=mesh,
        in_specs=(
            P("fsdp", None, "tile", None),
            P("tile", None),
            P(),
            P(),
            P(None, "fsdp"),
            P("fsdp", None),
            P("fsdp", None, "tile", None),
        ),
        out_specs=(
            P("fsdp", None, "tile", None),
            P("fsdp", None, "tile", None),
            P(),
            P(),
            P(None, "fsdp"),
            P("fsdp", None),
        ),
        check_vma=False,
    )
```

```python
import functools
import math

import jax
import jax.numpy as jnp
from jax import lax
from jax.experimental import pallas as pl
from jax.experimental.pallas import tpu as pltpu
from jax.sharding import PartitionSpec as P

MESH = pl.DeviceIdType.MESH
F32 = jnp.float32
BF16 = jnp.bfloat16

eps = 1e-06
inv_root2 = 0.7071067811865476
inv_root_tau = 0.3989422804014327

TOP = 8


def dot(lhs, rhs, dims=(((1,), (0,)), ((), ()))):
    return lax.dot_general(lhs, rhs, dims, preferred_element_type=F32)


def kernel_body(
    tiles, hi, height, width, channels, factor, n_sems,
    x_hbm, seam_ref, kern_hbm, gain_hbm, win_hbm, wout_hbm, cot_hbm,
    mixed_hbm, fgrad_hbm, kgrad_hbm, ggrad_hbm, wing_hbm, woutg_hbm,
    ext, dpad, flip, flip2, tmp, normed, rstd_ref, own_ds, keep_ds, own_br, keep_br, hid, dpre, hid_t, sc_t, win_t, wout_t, pre_ref, dhid_ref,
    hs, hr, adj_s, adj_r, core,
    sc_all, cot_all, ds_s, ds_r, br_s, br_r,
    gf, gs, xr, part, zs, zr, agz, agx,
    kfull, kr, kl, klr, kz, kf,
    x_ref, kern_ref, gain_ref, win_ref, wout_ref, cot_ref,
    mixed_ref, fgrad_ref, kgrad_ref, ggrad_ref, wing_ref, woutg_ref,
    load_sems, store_sems, send_sems, recv_sems,
):
    pairs = (
        (x_hbm, x_ref), (cot_hbm, cot_ref), (kern_hbm, kern_ref), (gain_hbm, gain_ref),
        (wout_hbm, wout_ref), (win_hbm, win_ref),
    )
    loads = [
        pltpu.make_async_copy(src, dst, load_sems.at[i]) for i, (src, dst) in enumerate(pairs)
    ]
    for load in loads:
        load.start()
    stores = []

    def store(src, dst):
        stores.append(pltpu.make_async_copy(src, dst, store_sems.at[len(stores)]))
        stores[-1].start()

    cells = height * width
    half = channels // 4
    t = lax.axis_index("tile")
    f = lax.axis_index("fsdp")
    west = lax.rem(t + tiles - 1, tiles)
    east = lax.rem(t + 1, tiles)
    x = lax.rem(t, 2)
    z = t // 2
    x_peer = z * 2 + (1 - x)
    z_at = [lax.rem(z + r, hi) for r in range(hi)]
    z_from = [lax.rem(z + hi - r, hi) for r in range(hi)]
    z_peer = [at * 2 + x for at in z_at]
    f_peer = [f, f + 1 - 2 * lax.rem(f, 2), lax.rem(f + 2, 4), 3 - f]

    barrier = pltpu.get_barrier_semaphore()
    greet = (
        [{"fsdp": f_peer[r]} for r in (1, 2, 3)]
        + [{"tile": west}, {"tile": east}, {"tile": x_peer}]
        + [{"tile": z_peer[r]} for r in range(1, hi)]
    )
    for device in greet:
        pl.semaphore_signal(barrier, inc=1, device_id=device, device_id_type=MESH)

    started = []

    def send(src, dst, device):
        index = len(started)
        copy = pltpu.make_async_remote_copy(
            src_ref=src, dst_ref=dst, send_sem=send_sems.at[index],
            recv_sem=recv_sems.at[index], device_id=device, device_id_type=MESH,
        )
        copy.start()
        started.append(copy)
        return index

    def arrived(index, ref):
        pltpu.make_async_remote_copy(
            src_ref=ref, dst_ref=ref, send_sem=send_sems.at[index],
            recv_sem=recv_sems.at[index], device_id={"tile": t, "fsdp": f}, device_id_type=MESH,
        ).wait_recv()

    def rows_of(j):
        return pl.ds(j * height, height)

    groups = [slice(128 * g, 128 * g + 128) for g in range(channels // 128)]

    def spread(ref, by_lanes):
        for g, lanes in enumerate(groups):
            by_lanes[g] = ref[:, lanes].astype(F32)

    def column_of(by_lanes, j):
        return jnp.concatenate(
            [by_lanes[g, pl.ds(j, height, stride=width), :] for g in range(len(groups))], axis=1
        )

    def put_column(by_lanes, j, value):
        for g, lanes in enumerate(groups):
            by_lanes[g, pl.ds(j, height, stride=width), :] = value[:, lanes]

    def gather_lanes(by_lanes, ref):
        for g, lanes in enumerate(groups):
            ref[:, lanes] = by_lanes[g].astype(BF16)

    loads[0].wait()
    spread(x_ref, flip)
    for j in range(width):
        column = column_of(flip, j)
        ext[3 + j, TOP : TOP + height, :] = column
        if j < 3:
            hs[0, rows_of(j), :] = column.astype(BF16)
        if j >= width - 3:
            hs[1, rows_of(j - width + 3), :] = column.astype(BF16)
    pl.semaphore_wait(barrier, len(greet))
    halo_w = send(hs.at[0], hr.at[1], {"tile": west})
    halo_e = send(hs.at[1], hr.at[0], {"tile": east})
    loads[1].wait()
    spread(cot_ref, flip2)
    for j in range(width):
        cot_all[0, rows_of(j), :] = column_of(flip2, j).astype(BF16)
    sibling = {"fsdp": f_peer[1]}
    across = {"fsdp": f_peer[2]}
    cot_id = [
        None,
        send(cot_all.at[0], cot_all.at[1], sibling),
        send(cot_all.at[0], cot_all.at[2], across),
        None,
    ]
    bottom = ext.shape[1] - TOP - height
    ext[:, 0:TOP, :] = jnp.zeros((width + 6, TOP, channels), F32)
    ext[:, TOP + height :, :] = jnp.zeros((width + 6, bottom, channels), F32)
    dpad[:, 0:TOP, :] = jnp.zeros((width, TOP, channels), F32)
    dpad[:, TOP + height :, :] = jnp.zeros((width, bottom, channels), F32)

    row_at = lax.broadcasted_iota(jnp.int32, (height, height), 0)
    col_at = lax.broadcasted_iota(jnp.int32, (height, height), 1)

    def picker(offset):
        return jnp.where(col_at == row_at + offset, 1.0, 0.0).astype(BF16)

    def lanes_of(g):
        return pl.ds(pl.multiple_of(g * 128, 128), 128)

    def conv_part(columns, fresh):
        @pl.loop(0, channels // 128)
        def _(g):
            lanes = lanes_of(g)
            total = [
                jnp.zeros((height, 128), F32) if fresh else tmp[rows_of(j), lanes]
                for j in range(width)
            ]
            for a in range(7):
                first = TOP - 3 + a
                shifted = {c: ext[c, first : first + height, lanes] for c in columns}
                for b in range(7):
                    tap = kern_ref[pl.ds(7 * a + b, 1), lanes]
                    for j in range(width):
                        if j + b in shifted:
                            total[j] = total[j] + shifted[j + b] * tap
            for j in range(width):
                tmp[rows_of(j), lanes] = total[j]

    loads[2].wait()
    conv_part(list(range(3, width + 3)), True)
    arrived(halo_w, hr.at[1])
    arrived(halo_e, hr.at[0])
    for side, first in ((0, 0), (1, width + 3)):
        pick = picker(seam_ref[0, side])
        for j in range(3):
            ext[first + j, TOP : TOP + height, :] = dot(pick, hr[side, rows_of(j), :])
    conv_part([0, 1, 2, width + 3, width + 4, width + 5], False)

    loads[3].wait()
    gain = gain_ref[...]

    @pl.loop(0, width)
    def _(j):
        at = pl.ds(pl.multiple_of(j * height, height), height)
        rows = tmp[at, :]
        centered = rows - jnp.mean(rows, axis=-1, keepdims=True)
        rstd = lax.rsqrt(jnp.mean(centered * centered, axis=-1, keepdims=True) + eps)
        unit = centered * rstd
        normed[at, :] = unit
        rstd_ref[at, :] = jnp.broadcast_to(rstd, (height, 128))
        sc_all[0, at, :] = (unit * gain).astype(BF16)

    sc_id = [
        None,
        send(sc_all.at[0], sc_all.at[1], sibling),
        send(sc_all.at[0], sc_all.at[2], across),
        None,
    ]
    loads[4].wait()
    loads[5].wait()
    w_in = win_ref[...]
    w_out = wout_ref[...]
    wout_t[...] = w_out.T
    win_t[...] = w_in.T
    ds_id = [None] * 4
    for r in range(4):
        if r > 0:
            arrived(cot_id[r], cot_all.at[r])
        if r == 2:
            cot_id[3] = send(cot_all.at[2], cot_all.at[3], sibling)
        dhid_ref[...] = dot(cot_all[r], wout_t[...])
        if r > 0:
            arrived(sc_id[r], sc_all.at[r])
        if r == 2:
            sc_id[3] = send(sc_all.at[2], sc_all.at[3], sibling)
        pre_ref[...] = dot(sc_all[r], w_in)

        @pl.loop(0, width)
        def _(j):
            at = pl.ds(pl.multiple_of(j * height, height), height)
            pre = pre_ref[at, :]
            phi = 0.5 * (1.0 + lax.erf(pre * inv_root2))
            slope = phi + pre * inv_root_tau * jnp.exp(-0.5 * pre * pre)
            hid[r, at, :] = (pre * phi).astype(BF16)
            dpre[r, at, :] = (dhid_ref[at, :] * slope).astype(BF16)

        back = dot(dpre[r], win_t[...])
        if r == 0:
            own_ds[...] = back
        elif r == 2:
            keep_ds[...] = back
        else:
            slot = r // 2
            ds_s[slot] = back.astype(BF16)
            ds_id[r] = send(ds_s.at[slot], ds_r.at[slot], sibling)
        own_cells = slice(r * cells, r * cells + cells)
        hid_t[:, own_cells] = hid[r].T
        if r < 3:
            sc_t[:, own_cells] = sc_all[r].T

    def term_start(h):
        lhs, rhs = ((hid_t, cot_all), (sc_t, dpre))[h // 2]
        lanes = slice((h % 2) * 2 * half, (h % 2) * 2 * half + 2 * half)
        total = dot(lhs[...], rhs[:, :, lanes].reshape(4 * cells, 2 * half))
        for side in range(2):
            gf[h, side] = total[:, side * half : (side + 1) * half]
            gs[h, side] = total[:, side * half : (side + 1) * half].astype(BF16)
        return send(gs.at[h, 1 - x], xr.at[h], {"tile": x_peer})

    piece = channels // hi

    def term_mid(h, index):
        arrived(index, xr.at[h])
        part[h] = gf[h, x] + xr[h].astype(F32)
        for r in range(1, hi):
            zs[h, r] = part[h, pl.ds(pl.multiple_of(z_at[r] * piece, piece), piece), :].astype(BF16)
        return [None] + [
            send(zs.at[h, r], zr.at[h, r], {"tile": z_peer[r]}) for r in range(1, hi)
        ]

    def term_sum(h, ids):
        total = part[h, pl.ds(pl.multiple_of(z * piece, piece), piece), :]
        for r in range(1, hi):
            arrived(ids[r], zr.at[h, r])
            total = total + zr[h, r].astype(F32)
        agz[h, z] = (total * factor).astype(BF16)
        return [None] + [
            send(agz.at[h, z], agz.at[h, z], {"tile": z_peer[r]}) for r in range(1, hi)
        ]

    def term_spread(h, ids):
        for r in range(1, hi):
            arrived(ids[r], agz.at[h, z_from[r]])
        return send(agz.at[h], agx.at[h], {"tile": x_peer})

    def term_put(h, side, value):
        ref = (woutg_ref, wing_ref)[h // 2]
        lanes = pl.ds(pl.multiple_of(((h % 2) * 2 + side) * half, half), half)
        ref[:, lanes] = value.astype(F32).reshape(channels, half)

    def term_end(h, index):
        arrived(index, agx.at[h])
        term_put(h, 1 - x, agx[h])

    x_ids, z_ids, g_ids, last = [None] * 4, [None] * 4, [None] * 4, [None] * 4
    x_ids[0] = term_start(0)

    arrived(ds_id[3], ds_r.at[1])
    ds_s[2] = (keep_ds[...] + ds_r[1].astype(F32)).astype(BF16)
    ds_id[2] = send(ds_s.at[2], ds_r.at[2], across)

    x_ids[1] = term_start(1)
    sc_t[:, 3 * cells :] = sc_all[3].T
    x_ids[2] = term_start(2)
    x_ids[3] = term_start(3)

    br_id = [None] * 4
    for r in (3, 1, 2, 0):
        branch = dot(hid[r], w_out)
        if r == 0:
            own_br[...] = branch
        elif r == 2:
            keep_br[...] = branch
        else:
            slot = r // 2
            br_s[slot] = branch.astype(BF16)
            br_id[r] = send(br_s.at[slot], br_r.at[slot], sibling)

    z_ids[0] = term_mid(0, x_ids[0])
    z_ids[1] = term_mid(1, x_ids[1])
    arrived(ds_id[1], ds_r.at[0])
    arrived(ds_id[2], ds_r.at[2])

    def norm_back(j, term_gain):
        at = pl.ds(pl.multiple_of(j * height, height), height)
        d_scaled = own_ds[at, :]
        for r in (0, 2):
            d_scaled = d_scaled + ds_r[r, at, :].astype(F32)
        unit = normed[at, :]
        both = d_scaled * unit
        g = d_scaled * gain
        mean_g = jnp.mean(g, axis=-1, keepdims=True)
        mean_gn = jnp.mean(g * unit, axis=-1, keepdims=True)
        dpad[j, TOP : TOP + height, :] = (g - mean_g - unit * mean_gn) * rstd_ref[at, 0:1]
        return term_gain + jnp.sum(both.reshape(height // 8, 8, channels), axis=0)

    term_gain = lax.fori_loop(0, width, norm_back, jnp.zeros((8, channels), F32))
    z_ids[2] = term_mid(2, x_ids[2])

    def adjoint(columns):
        @pl.loop(0, channels // 128)
        def _(g):
            lanes = lanes_of(g)
            total = {c: jnp.zeros((height, 128), F32) for c in columns}
            for a in range(7):
                first = TOP + 3 - a
                shifted = [dpad[j, first : first + height, lanes] for j in range(width)]
                for b in range(7):
                    tap = kern_ref[pl.ds(7 * a + b, 1), lanes]
                    for j in range(width):
                        if j + b in total:
                            total[j + b] = total[j + b] + shifted[j] * tap
            for c in columns:
                core[c, :, lanes] = total[c]

    adjoint([0, 1, 2, width + 3, width + 4, width + 5])
    for side, first in ((0, 0), (1, width + 3)):
        pick = picker(-seam_ref[0, side])
        for j in range(3):
            adj_s[side, rows_of(j), :] = dot(pick, core[first + j].astype(BF16)).astype(BF16)
    adj_w = send(adj_s.at[0], adj_r.at[1], {"tile": west})
    adj_e = send(adj_s.at[1], adj_r.at[0], {"tile": east})
    z_ids[3] = term_mid(3, x_ids[3])

    kfull[3] = jnp.zeros((16, channels), F32)
    kfull[3, 1:2, :] = jnp.sum(term_gain, axis=0, keepdims=True)

    @pl.loop(0, channels // 128)
    def _(g):
        lanes = lanes_of(g)
        d_here = dpad[:, TOP : TOP + height, lanes]
        for a in range(7):
            shifted = ext[:, TOP - 3 + a : TOP - 3 + a + height, lanes]
            for b in range(7):
                tap = 7 * a + b
                both = (d_here * shifted[b : b + width]).reshape(cells // 8, 8, 128)
                column = jnp.sum(jnp.sum(both, axis=0), axis=0, keepdims=True)
                kfull[tap // 16, tap % 16 : tap % 16 + 1, lanes] = column

    kr_id = [None] + [
        send(kfull.at[f_peer[r]], kr.at[r - 1], {"fsdp": f_peer[r]}) for r in (1, 2, 3)
    ]
    g_ids[0] = term_sum(0, z_ids[0])
    g_ids[1] = term_sum(1, z_ids[1])

    arrived(br_id[3], br_r.at[1])
    br_s[2] = (keep_br[...] + br_r[1].astype(F32)).astype(BF16)
    br_id[2] = send(br_s.at[2], br_r.at[2], across)

    total = kfull[f]
    for r in (1, 2, 3):
        arrived(kr_id[r], kr.at[r - 1])
        total = total + kr[r - 1]
    kl[...] = total
    kl_id = send(kl, klr, {"tile": x_peer})
    g_ids[2] = term_sum(2, z_ids[2])

    adjoint(list(range(3, width + 3)))

    arrived(kl_id, klr)
    kz[z] = kl[...] + klr[...]
    kz_id = [None] + [send(kz.at[z], kz.at[z], {"tile": z_peer[r]}) for r in range(1, hi)]
    g_ids[3] = term_sum(3, z_ids[3])
    last[0] = term_spread(0, g_ids[0])
    last[1] = term_spread(1, g_ids[1])

    arrived(adj_w, adj_r.at[1])
    arrived(adj_e, adj_r.at[0])
    for j in range(width):
        value = cot_all[0, rows_of(j), :].astype(F32) + core[3 + j]
        if j < 3:
            value = value + adj_r[0, rows_of(j), :].astype(F32)
        if j >= width - 3:
            value = value + adj_r[1, rows_of(j - width + 3), :].astype(F32)
        put_column(flip, j, value)
    gather_lanes(flip, fgrad_ref)
    store(fgrad_ref, fgrad_hbm)

    for r in range(1, hi):
        arrived(kz_id[r], kz.at[z_from[r]])
    total = kz[0]
    for at in range(1, hi):
        total = total + kz[at]
    kf[f] = total * factor
    kf_id = [None] + [send(kf.at[f], kf.at[f], {"fsdp": f_peer[r]}) for r in (1, 2, 3)]

    last[2] = term_spread(2, g_ids[2])

    arrived(br_id[1], br_r.at[0])
    arrived(br_id[2], br_r.at[2])
    for j in range(width):
        at = rows_of(j)
        value = ext[3 + j, TOP : TOP + height, :] + own_br[at, :]
        for r in (0, 2):
            value = value + br_r[r, at, :].astype(F32)
        put_column(flip2, j, value)
    gather_lanes(flip2, mixed_ref)
    store(mixed_ref, mixed_hbm)

    last[3] = term_spread(3, g_ids[3])

    for r in (1, 2, 3):
        arrived(kf_id[r], kf.at[f_peer[r]])
    for at in range(3):
        kgrad_ref[16 * at : 16 * at + 16, :] = kf[at]
    kgrad_ref[48:49, :] = kf[3, 0:1, :]
    ggrad_ref[...] = kf[3, 1:2, :]
    store(kgrad_ref, kgrad_hbm)
    store(ggrad_ref, ggrad_hbm)

    for h in range(4):
        term_put(h, x, agz[h])
    for h in range(4):
        term_end(h, last[h])
        if h == 1:
            store(woutg_ref, woutg_hbm)
    store(wing_ref, wing_hbm)
    for copy in stores:
        copy.wait()
    for copy in started:
        copy.wait_send()
    assert len(started) <= n_sems


def write_out(*refs):
    count = (len(refs) - 2) // 3
    sources, targets, held = (refs[i * count : i * count + count] for i in range(3))
    in_sems, out_sems = refs[-2:]
    loads = [pltpu.make_async_copy(sources[i], held[i], in_sems.at[i]) for i in range(count)]
    stores = [pltpu.make_async_copy(held[i], targets[i], out_sems.at[i]) for i in range(count)]
    for load in loads:
        load.start()
    for load, save in zip(loads, stores):
        load.wait()
        save.start()
    for save in stores:
        save.wait()


def body(tiles, shards, fields, seam_shift, kernel, gain, w_in, w_out, cotangent):
    _, height, width, channels = fields.shape
    cells = height * width
    hidden = w_in.shape[1]
    assert shards == 4 and tiles % 2 == 0 and kernel.shape[0] == 49
    assert hidden == channels and channels % (16 * (tiles // 2)) == 0
    hi = tiles // 2
    factor = 1.0 / math.sqrt(cells * tiles * shards)
    half = channels // 4
    piece = channels // hi
    n_sems = 32 + 4 * (2 + 2 * (hi - 1)) + hi
    padded = height + 16

    def vmem(shape, kind):
        return pltpu.VMEM(shape, kind)

    away = pl.BlockSpec(memory_space=pltpu.HBM)
    rows = (cells, channels)
    outs = pl.pallas_call(
        functools.partial(kernel_body, tiles, hi, height, width, channels, factor, n_sems),
        out_shape=(
            jax.ShapeDtypeStruct(rows, BF16),
            jax.ShapeDtypeStruct(rows, BF16),
            jax.ShapeDtypeStruct(kernel.shape, F32),
            jax.ShapeDtypeStruct((1, channels), F32),
            jax.ShapeDtypeStruct(w_in.shape, F32),
            jax.ShapeDtypeStruct(w_out.shape, F32),
        ),
        in_specs=[
            away, pl.BlockSpec(memory_space=pltpu.SMEM), away, away, away, away, away,
        ],
        out_specs=[away] * 6,
        scratch_shapes=[
            vmem((width + 6, padded, channels), F32),
            vmem((width, padded, channels), F32),
            vmem((channels // 128, cells, 128), F32),
            vmem((channels // 128, cells, 128), F32),
            vmem(rows, F32),
            vmem(rows, F32),
            vmem((cells, 128), F32),
            vmem(rows, F32),
            vmem(rows, F32),
            vmem(rows, F32),
            vmem(rows, F32),
            vmem((4, cells, hidden), BF16),
            vmem((4, cells, hidden), BF16),
            vmem((hidden, 4 * cells), BF16),
            vmem((channels, 4 * cells), BF16),
            vmem((hidden, channels), BF16),
            vmem((channels, hidden), BF16),
            vmem((cells, hidden), F32),
            vmem((cells, hidden), F32),
            vmem((2, 3 * height, channels), BF16),
            vmem((2, 3 * height, channels), BF16),
            vmem((2, 3 * height, channels), BF16),
            vmem((2, 3 * height, channels), BF16),
            vmem((width + 6, height, channels), F32),
            vmem((4, cells, channels), BF16),
            vmem((4, cells, channels), BF16),
            vmem((3, cells, channels), BF16),
            vmem((3, cells, channels), BF16),
            vmem((3, cells, channels), BF16),
            vmem((3, cells, channels), BF16),
            vmem((4, 2, channels, half), F32),
            vmem((4, 2, channels, half), BF16),
            vmem((4, channels, half), BF16),
            vmem((4, channels, half), F32),
            vmem((4, hi, piece, half), BF16),
            vmem((4, hi, piece, half), BF16),
            vmem((4, hi, piece, half), BF16),
            vmem((4, hi, piece, half), BF16),
            vmem((4, 16, channels), F32),
            vmem((3, 16, channels), F32),
            vmem((16, channels), F32),
            vmem((16, channels), F32),
            vmem((hi, 16, channels), F32),
            vmem((4, 16, channels), F32),
            vmem(rows, BF16),
            vmem(kernel.shape, F32),
            vmem((1, channels), F32),
            vmem(w_in.shape, BF16),
            vmem(w_out.shape, BF16),
            vmem(rows, BF16),
            vmem(rows, BF16),
            vmem(rows, BF16),
            vmem(kernel.shape, F32),
            vmem((1, channels), F32),
            vmem(w_in.shape, F32),
            vmem(w_out.shape, F32),
            pltpu.SemaphoreType.DMA((6,)),
            pltpu.SemaphoreType.DMA((6,)),
            pltpu.SemaphoreType.DMA((n_sems,)),
            pltpu.SemaphoreType.DMA((n_sems,)),
        ],
        compiler_params=pltpu.CompilerParams(
            collective_id=0, has_side_effects=True, vmem_limit_bytes=58 * 1024 * 1024
        ),
        name="block",
    )(
        fields.reshape(rows), seam_shift, kernel, gain.reshape(1, channels), w_in, w_out,
        cotangent.reshape(rows),
    )
    outs = pl.pallas_call(
        write_out,
        out_shape=[jax.ShapeDtypeStruct(out.shape, out.dtype) for out in outs],
        in_specs=[away] * 6,
        out_specs=[away] * 6,
        scratch_shapes=[pltpu.VMEM(out.shape, out.dtype) for out in outs]
        + [pltpu.SemaphoreType.DMA((6,)), pltpu.SemaphoreType.DMA((6,))],
        compiler_params=pltpu.CompilerParams(vmem_limit_bytes=58 * 1024 * 1024),
        name="write_out",
    )(*outs)
    mixed, field_grad, kernel_grad, gain_grad, w_in_grad, w_out_grad = outs
    return (
        mixed.reshape(fields.shape), field_grad.reshape(fields.shape), kernel_grad,
        gain_grad.reshape(channels), w_in_grad, w_out_grad,
    )


def solution(mesh):
    return jax.shard_map(
        functools.partial(body, mesh.shape["tile"], mesh.shape["fsdp"]),
        mesh=mesh,
        in_specs=(
            P("fsdp", None, "tile", None),
            P("tile", None),
            P(),
            P(),
            P(None, "fsdp"),
            P("fsdp", None),
            P("fsdp", None, "tile", None),
        ),
        out_specs=(
            P("fsdp", None, "tile", None),
            P("fsdp", None, "tile", None),
            P(),
            P(),
            P(None, "fsdp"),
            P("fsdp", None),
        ),
        check_vma=False,
    )
```

```python
import functools
import math

import jax
import jax.numpy as jnp
from jax import lax
from jax.experimental import pallas as pl
from jax.experimental.pallas import tpu as pltpu
from jax.sharding import PartitionSpec as P

MESH = pl.DeviceIdType.MESH
F32 = jnp.float32
BF16 = jnp.bfloat16

eps = 1e-06
inv_root2 = 0.7071067811865476
inv_root_tau = 0.3989422804014327

TOP = 8


def dot(lhs, rhs, dims=(((1,), (0,)), ((), ()))):
    return lax.dot_general(lhs, rhs, dims, preferred_element_type=F32)


def kernel_body(
    tiles, hi, height, width, channels, factor, n_sems,
    x_hbm, seam_ref, kern_hbm, gain_hbm, win_hbm, wout_hbm, cot_hbm,
    mixed_hbm, fgrad_hbm, kgrad_hbm, ggrad_hbm, wing_hbm, woutg_hbm,
    ext, dpad, flip, flip2, tmp, normed, rstd_ref, own_ds, keep_ds, own_br, keep_br, hid, dpre, hid_t, sc_t, win_t, wout_t, pre_ref, dhid_ref,
    hs, hr, adj_s, adj_r, core,
    sc_all, cot_all, ds_s, ds_r, br_s, br_r,
    gf, gs, xr, part, zs, zr, agz, agx,
    kfull, kr, kl, klr, kz, kf,
    x_ref, kern_ref, gain_ref, win_ref, wout_ref, cot_ref,
    mixed_ref, fgrad_ref, kgrad_ref, ggrad_ref, wing_ref, woutg_ref,
    load_sems, store_sems, send_sems, recv_sems,
):
    pairs = (
        (x_hbm, x_ref), (cot_hbm, cot_ref), (kern_hbm, kern_ref), (gain_hbm, gain_ref),
        (wout_hbm, wout_ref), (win_hbm, win_ref),
    )
    loads = [
        pltpu.make_async_copy(src, dst, load_sems.at[i]) for i, (src, dst) in enumerate(pairs)
    ]
    for load in loads:
        load.start()
    stores = []

    def store(src, dst):
        stores.append(pltpu.make_async_copy(src, dst, store_sems.at[len(stores)]))
        stores[-1].start()

    cells = height * width
    half = channels // 4
    piece = channels // hi
    t = lax.axis_index("tile")
    f = lax.axis_index("fsdp")
    west = lax.rem(t + tiles - 1, tiles)
    east = lax.rem(t + 1, tiles)
    x = lax.rem(t, 2)
    z = t // 2
    x_peer = z * 2 + (1 - x)
    z_at = [lax.rem(z + r, hi) for r in range(hi)]
    z_from = [lax.rem(z + hi - r, hi) for r in range(hi)]
    z_peer = [at * 2 + x for at in z_at]
    f_peer = [f, f + 1 - 2 * lax.rem(f, 2), lax.rem(f + 2, 4), 3 - f]

    barrier = pltpu.get_barrier_semaphore()
    greet = (
        [{"fsdp": f_peer[r]} for r in (1, 2, 3)]
        + [{"tile": west}, {"tile": east}, {"tile": x_peer}]
        + [{"tile": z_peer[r]} for r in range(1, hi)]
    )
    for device in greet:
        pl.semaphore_signal(barrier, inc=1, device_id=device, device_id_type=MESH)

    started = []

    def send(src, dst, device):
        index = len(started)
        copy = pltpu.make_async_remote_copy(
            src_ref=src, dst_ref=dst, send_sem=send_sems.at[index],
            recv_sem=recv_sems.at[index], device_id=device, device_id_type=MESH,
        )
        copy.start()
        started.append(copy)
        return index

    def arrived(index, ref):
        pltpu.make_async_remote_copy(
            src_ref=ref, dst_ref=ref, send_sem=send_sems.at[index],
            recv_sem=recv_sems.at[index], device_id={"tile": t, "fsdp": f}, device_id_type=MESH,
        ).wait_recv()

    def rows_of(j):
        return pl.ds(j * height, height)

    groups = [slice(128 * g, 128 * g + 128) for g in range(channels // 128)]

    def spread(ref, by_lanes):
        for g, lanes in enumerate(groups):
            by_lanes[g] = ref[:, lanes].astype(F32)

    def column_of(by_lanes, j):
        return jnp.concatenate(
            [by_lanes[g, pl.ds(j, height, stride=width), :] for g in range(len(groups))], axis=1
        )

    def put_column(by_lanes, j, value):
        for g, lanes in enumerate(groups):
            by_lanes[g, pl.ds(j, height, stride=width), :] = value[:, lanes]

    def gather_lanes(by_lanes, ref):
        for g, lanes in enumerate(groups):
            ref[:, lanes] = by_lanes[g].astype(BF16)

    loads[0].wait()
    spread(x_ref, flip)
    for j in range(width):
        column = column_of(flip, j)
        ext[3 + j, TOP : TOP + height, :] = column
        if j < 3:
            hs[0, rows_of(j), :] = column.astype(BF16)
        if j >= width - 3:
            hs[1, rows_of(j - width + 3), :] = column.astype(BF16)
    pl.semaphore_wait(barrier, len(greet))
    halo_w = send(hs.at[0], hr.at[1], {"tile": west})
    halo_e = send(hs.at[1], hr.at[0], {"tile": east})
    loads[1].wait()
    spread(cot_ref, flip2)
    for j in range(width):
        cot_all[0, rows_of(j), :] = column_of(flip2, j).astype(BF16)
    sibling = {"fsdp": f_peer[1]}
    across = {"fsdp": f_peer[2]}
    cot_id = [
        None,
        send(cot_all.at[0], cot_all.at[1], sibling),
        send(cot_all.at[0], cot_all.at[2], across),
        None,
    ]
    bottom = ext.shape[1] - TOP - height
    ext[:, 0:TOP, :] = jnp.zeros((width + 6, TOP, channels), F32)
    ext[:, TOP + height :, :] = jnp.zeros((width + 6, bottom, channels), F32)
    dpad[:, 0:TOP, :] = jnp.zeros((width, TOP, channels), F32)
    dpad[:, TOP + height :, :] = jnp.zeros((width, bottom, channels), F32)

    row_at = lax.broadcasted_iota(jnp.int32, (height, height), 0)
    col_at = lax.broadcasted_iota(jnp.int32, (height, height), 1)

    def picker(offset):
        return jnp.where(col_at == row_at + offset, 1.0, 0.0).astype(BF16)

    def lanes_of(g):
        return pl.ds(pl.multiple_of(g * 128, 128), 128)

    def conv_part(columns, fresh):
        @pl.loop(0, channels // 128)
        def _(g):
            lanes = lanes_of(g)
            total = [
                jnp.zeros((height, 128), F32) if fresh else tmp[rows_of(j), lanes]
                for j in range(width)
            ]
            for a in range(7):
                first = TOP - 3 + a
                shifted = {c: ext[c, first : first + height, lanes] for c in columns}
                for b in range(7):
                    tap = kern_ref[pl.ds(7 * a + b, 1), lanes]
                    for j in range(width):
                        if j + b in shifted:
                            total[j] = total[j] + shifted[j + b] * tap
            for j in range(width):
                tmp[rows_of(j), lanes] = total[j]

    loads[2].wait()
    conv_part(list(range(3, width + 3)), True)
    arrived(halo_w, hr.at[1])
    arrived(halo_e, hr.at[0])
    for side, first in ((0, 0), (1, width + 3)):
        pick = picker(seam_ref[0, side])
        for j in range(3):
            ext[first + j, TOP : TOP + height, :] = dot(pick, hr[side, rows_of(j), :])
    conv_part([0, 1, 2, width + 3, width + 4, width + 5], False)

    loads[3].wait()
    gain = gain_ref[...]

    sibling_sc, across_sc = [None] * 2, [None] * 2
    part_rows = [pl.ds(p * (cells // 2), cells // 2) for p in range(2)]
    for p in range(2):

        @pl.loop(p * (width // 2), (p + 1) * (width // 2))
        def _(j):
            at = pl.ds(pl.multiple_of(j * height, height), height)
            rows = tmp[at, :]
            centered = rows - jnp.mean(rows, axis=-1, keepdims=True)
            rstd = lax.rsqrt(jnp.mean(centered * centered, axis=-1, keepdims=True) + eps)
            unit = centered * rstd
            normed[at, :] = unit
            rstd_ref[at, :] = jnp.broadcast_to(rstd, (height, 128))
            sc_all[0, at, :] = (unit * gain).astype(BF16)

        across_sc[p] = send(sc_all.at[0, part_rows[p]], sc_all.at[2, part_rows[p]], across)
    sibling_sc = send(sc_all.at[0], sc_all.at[1], sibling)
    forward_sc = [None] * 2
    loads[4].wait()
    loads[5].wait()
    w_in = win_ref[...]
    w_out = wout_ref[...]
    wout_t[...] = w_out.T
    win_t[...] = w_in.T
    def term_start(h):
        lhs, rhs = ((hid_t, cot_all), (sc_t, dpre))[h // 2]
        lanes = slice((h % 2) * 2 * half, (h % 2) * 2 * half + 2 * half)
        total = dot(lhs[...], rhs[:, :, lanes].reshape(4 * cells, 2 * half))
        for side in range(2):
            gf[h, side] = total[:, side * half : (side + 1) * half]
            gs[h, side] = total[:, side * half : (side + 1) * half].astype(BF16)
        return send(gs.at[h, 1 - x], xr.at[h], {"tile": x_peer})

    def term_mid(h, index):
        arrived(index, xr.at[h])
        part[h] = gf[h, x] + xr[h].astype(F32)
        for r in range(1, hi):
            zs[h, r] = part[h, pl.ds(pl.multiple_of(z_at[r] * piece, piece), piece), :].astype(BF16)
        return [None] + [
            send(zs.at[h, r], zr.at[h, r], {"tile": z_peer[r]}) for r in range(1, hi)
        ]

    def term_sum(h, ids):
        total = part[h, pl.ds(pl.multiple_of(z * piece, piece), piece), :]
        for r in range(1, hi):
            arrived(ids[r], zr.at[h, r])
            total = total + zr[h, r].astype(F32)
        agz[h, z] = (total * factor).astype(BF16)
        ids = [None] + [
            send(agz.at[h, z], agz.at[h, z], {"tile": z_peer[r]}) for r in range(1, hi)
        ]
        last[h] = [send(agz.at[h, z], agx.at[h, z], {"tile": x_peer})]
        return ids

    def term_put(h, side, value):
        ref, target = ((woutg_ref, woutg_hbm), (wing_ref, wing_hbm))[h // 2]
        lanes = pl.ds(pl.multiple_of(((h % 2) * 2 + side) * half, half), half)
        ref[:, lanes] = value.astype(F32).reshape(channels, half)
        store(ref.at[:, lanes], target.at[:, lanes])

    def term_spread(h, ids):
        for r in range(1, hi):
            arrived(ids[r], agz.at[h, z_from[r]])
            last[h].append(
                send(agz.at[h, z_from[r]], agx.at[h, z_from[r]], {"tile": x_peer})
            )
        term_put(h, x, agz[h])

    def term_end(h):
        for r in range(hi):
            arrived(last[h][r], agx.at[h, z_from[r]])
        term_put(h, 1 - x, agx[h])

    ds_id = [None] * 4
    x_ids, z_ids, g_ids, last = [None] * 4, [None] * 4, [None] * 4, [None] * 4

    def units(r, p):
        rows = part_rows[p]
        pre_ref[rows, :] = dot(sc_all[r, rows, :], w_in)

        @pl.loop(p * (width // 2), (p + 1) * (width // 2))
        def _(j):
            at = pl.ds(pl.multiple_of(j * height, height), height)
            pre = pre_ref[at, :]
            phi = 0.5 * (1.0 + lax.erf(pre * inv_root2))
            slope = phi + pre * inv_root_tau * jnp.exp(-0.5 * pre * pre)
            hid[r, at, :] = (pre * phi).astype(BF16)
            dpre[r, at, :] = (dhid_ref[at, :] * slope).astype(BF16)

        own_cells = slice(r * cells + p * (cells // 2), r * cells + (p + 1) * (cells // 2))
        hid_t[:, own_cells] = hid[r, rows, :].T
        if r < 3:
            sc_t[:, own_cells] = sc_all[r, rows, :].T

    for r in range(4):
        if r > 0:
            arrived(cot_id[r], cot_all.at[r])
        if r == 2:
            cot_id[3] = send(cot_all.at[2], cot_all.at[3], sibling)
        dhid_ref[...] = dot(cot_all[r], wout_t[...])
        if r == 1:
            arrived(sibling_sc, sc_all.at[1])
        for p in range(2):
            if r == 2:
                arrived(across_sc[p], sc_all.at[2, part_rows[p]])
                forward_sc[p] = send(sc_all.at[2, part_rows[p]], sc_all.at[3, part_rows[p]], sibling)
            if r == 3:
                arrived(forward_sc[p], sc_all.at[3, part_rows[p]])
            units(r, p)
        if r == 3:
            x_ids[0] = term_start(0)
        back = dot(dpre[r], win_t[...])
        if r == 0:
            own_ds[...] = back
        elif r == 2:
            keep_ds[...] = back
        else:
            slot = r // 2
            ds_s[slot] = back.astype(BF16)
            ds_id[r] = send(ds_s.at[slot], ds_r.at[slot], sibling)

    x_ids[1] = term_start(1)
    arrived(ds_id[3], ds_r.at[1])
    ds_s[2] = (keep_ds[...] + ds_r[1].astype(F32)).astype(BF16)
    ds_id[2] = send(ds_s.at[2], ds_r.at[2], across)
    sc_t[:, 3 * cells :] = sc_all[3].T
    x_ids[2] = term_start(2)
    x_ids[3] = term_start(3)

    br_id = [None] * 4
    for r in (3, 2, 1, 0):
        branch = dot(hid[r], w_out)
        if r == 0:
            own_br[...] = branch
        elif r == 2:
            keep_br[...] = branch
        else:
            slot = r // 2
            br_s[slot] = branch.astype(BF16)
            br_id[r] = send(br_s.at[slot], br_r.at[slot], sibling)

    z_ids[0] = term_mid(0, x_ids[0])
    arrived(br_id[3], br_r.at[1])
    br_s[2] = (keep_br[...] + br_r[1].astype(F32)).astype(BF16)
    br_id[2] = send(br_s.at[2], br_r.at[2], across)
    z_ids[1] = term_mid(1, x_ids[1])
    g_ids[0] = term_sum(0, z_ids[0])
    arrived(ds_id[1], ds_r.at[0])
    arrived(ds_id[2], ds_r.at[2])

    def norm_back(j, term_gain):
        at = pl.ds(pl.multiple_of(j * height, height), height)
        d_scaled = own_ds[at, :]
        for r in (0, 2):
            d_scaled = d_scaled + ds_r[r, at, :].astype(F32)
        unit = normed[at, :]
        both = d_scaled * unit
        g = d_scaled * gain
        mean_g = jnp.mean(g, axis=-1, keepdims=True)
        mean_gn = jnp.mean(g * unit, axis=-1, keepdims=True)
        dpad[j, TOP : TOP + height, :] = (g - mean_g - unit * mean_gn) * rstd_ref[at, 0:1]
        return term_gain + jnp.sum(both.reshape(height // 8, 8, channels), axis=0)

    term_gain = lax.fori_loop(0, width, norm_back, jnp.zeros((8, channels), F32))
    z_ids[2] = term_mid(2, x_ids[2])

    def adjoint(columns):
        @pl.loop(0, channels // 128)
        def _(g):
            lanes = lanes_of(g)
            total = {c: jnp.zeros((height, 128), F32) for c in columns}
            for a in range(7):
                first = TOP + 3 - a
                shifted = [dpad[j, first : first + height, lanes] for j in range(width)]
                for b in range(7):
                    tap = kern_ref[pl.ds(7 * a + b, 1), lanes]
                    for j in range(width):
                        if j + b in total:
                            total[j + b] = total[j + b] + shifted[j] * tap
            for c in columns:
                core[c, :, lanes] = total[c]

    adjoint([0, 1, 2, width + 3, width + 4, width + 5])
    for side, first in ((0, 0), (1, width + 3)):
        pick = picker(-seam_ref[0, side])
        for j in range(3):
            adj_s[side, rows_of(j), :] = dot(pick, core[first + j].astype(BF16)).astype(BF16)
    adj_w = send(adj_s.at[0], adj_r.at[1], {"tile": west})
    adj_e = send(adj_s.at[1], adj_r.at[0], {"tile": east})
    z_ids[3] = term_mid(3, x_ids[3])

    kfull[3] = jnp.zeros((16, channels), F32)
    kfull[3, 1:2, :] = jnp.sum(term_gain, axis=0, keepdims=True)
    g_ids[1] = term_sum(1, z_ids[1])

    def tap_sums(first_group, last_group):
        @pl.loop(first_group, last_group)
        def _(g):
            lanes = lanes_of(g)
            d_here = dpad[:, TOP : TOP + height, lanes]
            for a in range(7):
                shifted = ext[:, TOP - 3 + a : TOP - 3 + a + height, lanes]
                for b in range(7):
                    tap = 7 * a + b
                    both = (d_here * shifted[b : b + width]).reshape(cells // 8, 8, 128)
                    column = jnp.sum(jnp.sum(both, axis=0), axis=0, keepdims=True)
                    kfull[tap // 16, tap % 16 : tap % 16 + 1, lanes] = column

    tap_sums(0, channels // 256)
    term_spread(0, g_ids[0])
    g_ids[2] = term_sum(2, z_ids[2])
    tap_sums(channels // 256, channels // 128)
    kr_id = [None] + [
        send(kfull.at[f_peer[r]], kr.at[r - 1], {"fsdp": f_peer[r]}) for r in (1, 2, 3)
    ]
    g_ids[3] = term_sum(3, z_ids[3])
    term_spread(1, g_ids[1])

    adjoint(list(range(3, width + 3)))

    total = kfull[f]
    for r in (1, 2, 3):
        arrived(kr_id[r], kr.at[r - 1])
        total = total + kr[r - 1]
    kl[...] = total
    kl_id = send(kl, klr, {"tile": x_peer})
    term_spread(2, g_ids[2])
    term_end(0)
    arrived(kl_id, klr)
    kz[z] = kl[...] + klr[...]
    kz_id = [None] + [send(kz.at[z], kz.at[z], {"tile": z_peer[r]}) for r in range(1, hi)]
    term_spread(3, g_ids[3])

    arrived(adj_w, adj_r.at[1])
    arrived(adj_e, adj_r.at[0])
    for j in range(width):
        value = cot_all[0, rows_of(j), :].astype(F32) + core[3 + j]
        if j < 3:
            value = value + adj_r[0, rows_of(j), :].astype(F32)
        if j >= width - 3:
            value = value + adj_r[1, rows_of(j - width + 3), :].astype(F32)
        put_column(flip, j, value)
    gather_lanes(flip, fgrad_ref)
    store(fgrad_ref, fgrad_hbm)

    for r in range(1, hi):
        arrived(kz_id[r], kz.at[z_from[r]])
    total = kz[0]
    for at in range(1, hi):
        total = total + kz[at]
    kf[f] = total * factor
    kf_id = [None] + [send(kf.at[f], kf.at[f], {"fsdp": f_peer[r]}) for r in (1, 2, 3)]

    term_end(1)
    arrived(br_id[1], br_r.at[0])
    arrived(br_id[2], br_r.at[2])
    for j in range(width):
        at = rows_of(j)
        value = ext[3 + j, TOP : TOP + height, :] + own_br[at, :]
        for r in (0, 2):
            value = value + br_r[r, at, :].astype(F32)
        put_column(flip2, j, value)
    gather_lanes(flip2, mixed_ref)
    store(mixed_ref, mixed_hbm)

    term_end(2)
    for r in (1, 2, 3):
        arrived(kf_id[r], kf.at[f_peer[r]])
    for at in range(3):
        kgrad_ref[16 * at : 16 * at + 16, :] = kf[at]
    kgrad_ref[48:49, :] = kf[3, 0:1, :]
    ggrad_ref[...] = kf[3, 1:2, :]
    store(kgrad_ref, kgrad_hbm)
    store(ggrad_ref, ggrad_hbm)

    term_end(3)
    for copy in stores:
        copy.wait()
    for copy in started:
        copy.wait_send()
    assert len(started) <= n_sems


def write_out(*refs):
    count = (len(refs) - 2) // 3
    sources, targets, held = (refs[i * count : i * count + count] for i in range(3))
    in_sems, out_sems = refs[-2:]
    loads = [pltpu.make_async_copy(sources[i], held[i], in_sems.at[i]) for i in range(count)]
    stores = [pltpu.make_async_copy(held[i], targets[i], out_sems.at[i]) for i in range(count)]
    for load in loads:
        load.start()
    for load, save in zip(loads, stores):
        load.wait()
        save.start()
    for save in stores:
        save.wait()


def body(tiles, shards, fields, seam_shift, kernel, gain, w_in, w_out, cotangent):
    _, height, width, channels = fields.shape
    cells = height * width
    hidden = w_in.shape[1]
    assert shards == 4 and tiles % 2 == 0 and kernel.shape[0] == 49
    assert hidden == channels and channels % (16 * (tiles // 2)) == 0
    hi = tiles // 2
    factor = 1.0 / math.sqrt(cells * tiles * shards)
    half = channels // 4
    piece = channels // hi
    n_sems = 32 + 4 * (1 + 2 * (hi - 1) + hi) + hi
    padded = height + 16

    def vmem(shape, kind):
        return pltpu.VMEM(shape, kind)

    away = pl.BlockSpec(memory_space=pltpu.HBM)
    rows = (cells, channels)
    outs = pl.pallas_call(
        functools.partial(kernel_body, tiles, hi, height, width, channels, factor, n_sems),
        out_shape=(
            jax.ShapeDtypeStruct(rows, BF16),
            jax.ShapeDtypeStruct(rows, BF16),
            jax.ShapeDtypeStruct(kernel.shape, F32),
            jax.ShapeDtypeStruct((1, channels), F32),
            jax.ShapeDtypeStruct(w_in.shape, F32),
            jax.ShapeDtypeStruct(w_out.shape, F32),
        ),
        in_specs=[
            away, pl.BlockSpec(memory_space=pltpu.SMEM), away, away, away, away, away,
        ],
        out_specs=[away] * 6,
        scratch_shapes=[
            vmem((width + 6, padded, channels), F32),
            vmem((width, padded, channels), F32),
            vmem((channels // 128, cells, 128), F32),
            vmem((channels // 128, cells, 128), F32),
            vmem(rows, F32),
            vmem(rows, F32),
            vmem((cells, 128), F32),
            vmem(rows, F32),
            vmem(rows, F32),
            vmem(rows, F32),
            vmem(rows, F32),
            vmem((4, cells, hidden), BF16),
            vmem((4, cells, hidden), BF16),
            vmem((hidden, 4 * cells), BF16),
            vmem((channels, 4 * cells), BF16),
            vmem((hidden, channels), BF16),
            vmem((channels, hidden), BF16),
            vmem((cells, hidden), F32),
            vmem((cells, hidden), F32),
            vmem((2, 3 * height, channels), BF16),
            vmem((2, 3 * height, channels), BF16),
            vmem((2, 3 * height, channels), BF16),
            vmem((2, 3 * height, channels), BF16),
            vmem((width + 6, height, channels), F32),
            vmem((4, cells, channels), BF16),
            vmem((4, cells, channels), BF16),
            vmem((3, cells, channels), BF16),
            vmem((3, cells, channels), BF16),
            vmem((3, cells, channels), BF16),
            vmem((3, cells, channels), BF16),
            vmem((4, 2, channels, half), F32),
            vmem((4, 2, channels, half), BF16),
            vmem((4, channels, half), BF16),
            vmem((4, channels, half), F32),
            vmem((4, hi, piece, half), BF16),
            vmem((4, hi, piece, half), BF16),
            vmem((4, hi, piece, half), BF16),
            vmem((4, hi, piece, half), BF16),
            vmem((4, 16, channels), F32),
            vmem((3, 16, channels), F32),
            vmem((16, channels), F32),
            vmem((16, channels), F32),
            vmem((hi, 16, channels), F32),
            vmem((4, 16, channels), F32),
            vmem(rows, BF16),
            vmem(kernel.shape, F32),
            vmem((1, channels), F32),
            vmem(w_in.shape, BF16),
            vmem(w_out.shape, BF16),
            vmem(rows, BF16),
            vmem(rows, BF16),
            vmem(rows, BF16),
            vmem(kernel.shape, F32),
            vmem((1, channels), F32),
            vmem(w_in.shape, F32),
            vmem(w_out.shape, F32),
            pltpu.SemaphoreType.DMA((6,)),
            pltpu.SemaphoreType.DMA((12,)),
            pltpu.SemaphoreType.DMA((n_sems,)),
            pltpu.SemaphoreType.DMA((n_sems,)),
        ],
        compiler_params=pltpu.CompilerParams(
            collective_id=0, has_side_effects=True, vmem_limit_bytes=58 * 1024 * 1024
        ),
        name="block",
    )(
        fields.reshape(rows), seam_shift, kernel, gain.reshape(1, channels), w_in, w_out,
        cotangent.reshape(rows),
    )
    outs = pl.pallas_call(
        write_out,
        out_shape=[jax.ShapeDtypeStruct(out.shape, out.dtype) for out in outs],
        in_specs=[away] * 6,
        out_specs=[away] * 6,
        scratch_shapes=[pltpu.VMEM(out.shape, out.dtype) for out in outs]
        + [pltpu.SemaphoreType.DMA((6,)), pltpu.SemaphoreType.DMA((6,))],
        compiler_params=pltpu.CompilerParams(vmem_limit_bytes=58 * 1024 * 1024),
        name="write_out",
    )(*outs)
    mixed, field_grad, kernel_grad, gain_grad, w_in_grad, w_out_grad = outs
    return (
        mixed.reshape(fields.shape), field_grad.reshape(fields.shape), kernel_grad,
        gain_grad.reshape(channels), w_in_grad, w_out_grad,
    )


def solution(mesh):
    return jax.shard_map(
        functools.partial(body, mesh.shape["tile"], mesh.shape["fsdp"]),
        mesh=mesh,
        in_specs=(
            P("fsdp", None, "tile", None),
            P("tile", None),
            P(),
            P(),
            P(None, "fsdp"),
            P("fsdp", None),
            P("fsdp", None, "tile", None),
        ),
        out_specs=(
            P("fsdp", None, "tile", None),
            P("fsdp", None, "tile", None),
            P(),
            P(),
            P(None, "fsdp"),
            P("fsdp", None),
        ),
        check_vma=False,
    )
```

```python
import functools
import math

import jax
import jax.numpy as jnp
from jax import lax
from jax.experimental import pallas as pl
from jax.experimental.pallas import tpu as pltpu
from jax.sharding import PartitionSpec as P

MESH = pl.DeviceIdType.MESH
F32 = jnp.float32
BF16 = jnp.bfloat16

eps = 1e-06
inv_root2 = 0.7071067811865476
inv_root_tau = 0.3989422804014327

TOP = 8


def dot(lhs, rhs, dims=(((1,), (0,)), ((), ()))):
    return lax.dot_general(lhs, rhs, dims, preferred_element_type=F32)


def kernel_body(
    tiles, hi, height, width, channels, factor, n_sems,
    x_hbm, seam_ref, kern_hbm, gain_hbm, win_hbm, wout_hbm, cot_hbm,
    mixed_hbm, fgrad_hbm, kgrad_hbm, ggrad_hbm, wg_hbm,
    ext, dpad, flip, flip2, tmp, normed, rstd_ref, own_ds, keep_ds, own_br, keep_br, hid, dpre, slopes, hid_t, sc_t, win_t, wout_t, pre_ref, dhid_ref,
    hs, hr, adj_s, adj_r, core,
    sc_all, cot_all, ds_s, ds_r, br_s, br_r,
    gf, gs, xr, part, zs, zr, agz, agx,
    kfull, kr, kl, klr, kz, kf,
    x_ref, kern_ref, gain_ref, win_ref, wout_ref, cot_ref,
    mixed_ref, fgrad_ref, kgrad_ref, ggrad_ref,
    load_sems, store_sems, send_sems, recv_sems,
):
    pairs = (
        (x_hbm, x_ref), (cot_hbm, cot_ref), (kern_hbm, kern_ref), (gain_hbm, gain_ref),
        (wout_hbm, wout_ref), (win_hbm, win_ref),
    )
    loads = [
        pltpu.make_async_copy(src, dst, load_sems.at[i]) for i, (src, dst) in enumerate(pairs)
    ]
    for load in loads:
        load.start()
    stores = []

    def store(src, dst):
        stores.append(pltpu.make_async_copy(src, dst, store_sems.at[len(stores)]))
        stores[-1].start()

    cells = height * width
    half = channels // 4
    piece = channels // hi
    t = lax.axis_index("tile")
    f = lax.axis_index("fsdp")
    west = lax.rem(t + tiles - 1, tiles)
    east = lax.rem(t + 1, tiles)
    x = lax.rem(t, 2)
    z = t // 2
    x_peer = z * 2 + (1 - x)
    z_at = [lax.rem(z + r, hi) for r in range(hi)]
    z_from = [lax.rem(z + hi - r, hi) for r in range(hi)]
    z_peer = [at * 2 + x for at in z_at]
    f_peer = [f, f + 1 - 2 * lax.rem(f, 2), lax.rem(f + 2, 4), 3 - f]

    barrier = pltpu.get_barrier_semaphore()
    greet = (
        [{"fsdp": f_peer[r]} for r in (1, 2, 3)]
        + [{"tile": west}, {"tile": east}, {"tile": x_peer}]
        + [{"tile": z_peer[r]} for r in range(1, hi)]
    )
    for device in greet:
        pl.semaphore_signal(barrier, inc=1, device_id=device, device_id_type=MESH)

    started = []

    def send(src, dst, device):
        index = len(started)
        copy = pltpu.make_async_remote_copy(
            src_ref=src, dst_ref=dst, send_sem=send_sems.at[index],
            recv_sem=recv_sems.at[index], device_id=device, device_id_type=MESH,
        )
        copy.start()
        started.append(copy)
        return index

    def arrived(index, ref):
        pltpu.make_async_remote_copy(
            src_ref=ref, dst_ref=ref, send_sem=send_sems.at[index],
            recv_sem=recv_sems.at[index], device_id={"tile": t, "fsdp": f}, device_id_type=MESH,
        ).wait_recv()

    def rows_of(j):
        return pl.ds(j * height, height)

    groups = [slice(128 * g, 128 * g + 128) for g in range(channels // 128)]

    def spread(ref, by_lanes):
        for g, lanes in enumerate(groups):
            by_lanes[g] = ref[:, lanes].astype(F32)

    def column_of(by_lanes, j):
        return jnp.concatenate(
            [by_lanes[g, pl.ds(j, height, stride=width), :] for g in range(len(groups))], axis=1
        )

    def put_column(by_lanes, j, value):
        for g, lanes in enumerate(groups):
            by_lanes[g, pl.ds(j, height, stride=width), :] = value[:, lanes]

    def gather_lanes(by_lanes, ref):
        for g, lanes in enumerate(groups):
            ref[:, lanes] = by_lanes[g].astype(BF16)

    loads[0].wait()
    spread(x_ref, flip)
    for j in range(width):
        column = column_of(flip, j)
        ext[3 + j, TOP : TOP + height, :] = column
        if j < 3:
            hs[0, rows_of(j), :] = column.astype(BF16)
        if j >= width - 3:
            hs[1, rows_of(j - width + 3), :] = column.astype(BF16)
    pl.semaphore_wait(barrier, len(greet))
    halo_w = send(hs.at[0], hr.at[1], {"tile": west})
    halo_e = send(hs.at[1], hr.at[0], {"tile": east})
    loads[1].wait()
    spread(cot_ref, flip2)
    for j in range(width):
        cot_all[0, rows_of(j), :] = column_of(flip2, j).astype(BF16)
    sibling = {"fsdp": f_peer[1]}
    across = {"fsdp": f_peer[2]}
    cot_id = [
        None,
        send(cot_all.at[0], cot_all.at[1], sibling),
        send(cot_all.at[0], cot_all.at[2], across),
        None,
    ]
    bottom = ext.shape[1] - TOP - height
    ext[:, 0:TOP, :] = jnp.zeros((width + 6, TOP, channels), F32)
    ext[:, TOP + height :, :] = jnp.zeros((width + 6, bottom, channels), F32)
    dpad[:, 0:TOP, :] = jnp.zeros((width, TOP, channels), F32)
    dpad[:, TOP + height :, :] = jnp.zeros((width, bottom, channels), F32)

    row_at = lax.broadcasted_iota(jnp.int32, (height, height), 0)
    col_at = lax.broadcasted_iota(jnp.int32, (height, height), 1)

    def picker(offset):
        return jnp.where(col_at == row_at + offset, 1.0, 0.0).astype(BF16)

    def lanes_of(g):
        return pl.ds(pl.multiple_of(g * 128, 128), 128)

    def conv_part(columns, fresh):
        @pl.loop(0, channels // 128)
        def _(g):
            lanes = lanes_of(g)
            reached = [j for j in range(width) if any(j <= c <= j + 6 for c in columns)]
            total = {
                j: jnp.zeros((height, 128), F32) if fresh else tmp[rows_of(j), lanes]
                for j in reached
            }
            for a in range(7):
                first = TOP - 3 + a
                shifted = {c: ext[c, first : first + height, lanes] for c in columns}
                for b in range(7):
                    tap = kern_ref[pl.ds(7 * a + b, 1), lanes]
                    for j in reached:
                        if j + b in shifted:
                            total[j] = total[j] + shifted[j + b] * tap
            for j in reached:
                tmp[rows_of(j), lanes] = total[j]

    loads[2].wait()
    conv_part(list(range(3, width + 3)), True)
    loads[3].wait()
    gain = gain_ref[...]
    sibling_sc, across_sc = [None] * 2, [None] * 2
    part_rows = [pl.ds(p * (cells // 2), cells // 2) for p in range(2)]
    for side, first in ((0, 0), (1, width + 3)):
        p = side
        arrived((halo_e, halo_w)[side], hr.at[side])
        pick = picker(seam_ref[0, side])
        for j in range(3):
            ext[first + j, TOP : TOP + height, :] = dot(pick, hr[side, rows_of(j), :])
        conv_part([first, first + 1, first + 2], False)

        @pl.loop(p * (width // 2), (p + 1) * (width // 2))
        def _(j):
            at = pl.ds(pl.multiple_of(j * height, height), height)
            rows = tmp[at, :]
            centered = rows - jnp.mean(rows, axis=-1, keepdims=True)
            rstd = lax.rsqrt(jnp.mean(centered * centered, axis=-1, keepdims=True) + eps)
            unit = centered * rstd
            normed[at, :] = unit
            rstd_ref[at, :] = jnp.broadcast_to(rstd, (height, 128))
            sc_all[0, at, :] = (unit * gain).astype(BF16)

        across_sc[p] = send(sc_all.at[0, part_rows[p]], sc_all.at[2, part_rows[p]], across)
    sibling_sc = send(sc_all.at[0], sc_all.at[1], sibling)
    forward_sc = [None] * 2
    loads[4].wait()
    loads[5].wait()
    w_in = win_ref[...]
    w_out = wout_ref[...]
    wout_t[...] = w_out.T
    win_t[...] = w_in.T
    def term_start(h):
        lhs, rhs = ((hid_t, cot_all), (sc_t, dpre))[h // 2]
        lanes = slice((h % 2) * 2 * half, (h % 2) * 2 * half + 2 * half)
        total = dot(lhs[...], rhs[:, :, lanes].reshape(4 * cells, 2 * half))
        for side in range(2):
            gf[h, side] = total[:, side * half : (side + 1) * half]
            gs[h, side] = total[:, side * half : (side + 1) * half].astype(BF16)
        return send(gs.at[h, 1 - x], xr.at[h], {"tile": x_peer})

    def term_mid(h, index):
        arrived(index, xr.at[h])
        part[h] = gf[h, x] + xr[h].astype(F32)
        for r in range(1, hi):
            zs[h, r] = part[h, pl.ds(pl.multiple_of(z_at[r] * piece, piece), piece), :].astype(BF16)
        return [None] + [
            send(zs.at[h, r], zr.at[h, r], {"tile": z_peer[r]}) for r in range(1, hi)
        ]

    def term_sum(h, ids):
        total = part[h, pl.ds(pl.multiple_of(z * piece, piece), piece), :]
        for r in range(1, hi):
            arrived(ids[r], zr.at[h, r])
            total = total + zr[h, r].astype(F32)
        agz[h, z] = (total * factor).astype(BF16)
        ids = [None] + [
            send(agz.at[h, z], agz.at[h, z], {"tile": z_peer[r]}) for r in range(1, hi)
        ]
        last[h] = [send(agz.at[h, z], agx.at[h, z], {"tile": x_peer})]
        return ids

    def term_spread(h, ids):
        for r in range(1, hi):
            arrived(ids[r], agz.at[h, z_from[r]])
            last[h].append(
                send(agz.at[h, z_from[r]], agx.at[h, z_from[r]], {"tile": x_peer})
            )
        store(agz.at[h], wg_hbm.at[h, x])

    def term_end(h):
        for r in range(hi):
            arrived(last[h][r], agx.at[h, z_from[r]])
        store(agx.at[h], wg_hbm.at[h, 1 - x])

    ds_id = [None] * 4
    x_ids, z_ids, g_ids, last = [None] * 4, [None] * 4, [None] * 4, [None] * 4

    def units(r, p):
        rows = part_rows[p]
        pre_ref[rows, :] = dot(sc_all[r, rows, :], w_in)

        @pl.loop(p * (width // 2), (p + 1) * (width // 2))
        def _(j):
            at = pl.ds(pl.multiple_of(j * height, height), height)
            pre = pre_ref[at, :]
            phi = 0.5 * (1.0 + lax.erf(pre * inv_root2))
            slopes[r % 2, at, :] = phi + pre * inv_root_tau * jnp.exp(-0.5 * pre * pre)
            hid[r, at, :] = (pre * phi).astype(BF16)

        own_cells = slice(r * cells + p * (cells // 2), r * cells + (p + 1) * (cells // 2))
        hid_t[:, own_cells] = hid[r, rows, :].T

    def units_back(r):
        dhid_ref[...] = dot(cot_all[r], wout_t[...])

        @pl.loop(0, width)
        def _(j):
            at = pl.ds(pl.multiple_of(j * height, height), height)
            dpre[r, at, :] = (dhid_ref[at, :] * slopes[r % 2, at, :]).astype(BF16)

        back = dot(dpre[r], win_t[...])
        if r == 0:
            own_ds[...] = back
        elif r == 2:
            keep_ds[...] = back
        else:
            slot = r // 2
            ds_s[slot] = back.astype(BF16)
            ds_id[r] = send(ds_s.at[slot], ds_r.at[slot], sibling)

    for r in (0, 1):
        if r == 1:
            arrived(cot_id[1], cot_all.at[1])
            arrived(sibling_sc, sc_all.at[1])
        for p in range(2):
            units(r, p)
        units_back(r)
        sc_t[:, r * cells : (r + 1) * cells] = sc_all[r].T
    arrived(cot_id[2], cot_all.at[2])
    cot_id[3] = send(cot_all.at[2], cot_all.at[3], sibling)
    for p in range(2):
        arrived(across_sc[p], sc_all.at[2, part_rows[p]])
        forward_sc[p] = send(sc_all.at[2, part_rows[p]], sc_all.at[3, part_rows[p]], sibling)
        units(2, p)
    for p in range(2):
        arrived(forward_sc[p], sc_all.at[3, part_rows[p]])
        units(3, p)
    arrived(cot_id[3], cot_all.at[3])
    x_ids[0] = term_start(0)
    units_back(3)
    x_ids[1] = term_start(1)
    units_back(2)
    arrived(ds_id[3], ds_r.at[1])
    ds_s[2] = (keep_ds[...] + ds_r[1].astype(F32)).astype(BF16)
    ds_id[2] = send(ds_s.at[2], ds_r.at[2], across)
    for r in (2, 3):
        sc_t[:, r * cells : (r + 1) * cells] = sc_all[r].T
    x_ids[2] = term_start(2)
    x_ids[3] = term_start(3)

    br_id = [None] * 4
    for r in (3, 2, 1, 0):
        branch = dot(hid[r], w_out)
        if r == 0:
            own_br[...] = branch
        elif r == 2:
            keep_br[...] = branch
        else:
            slot = r // 2
            br_s[slot] = branch.astype(BF16)
            br_id[r] = send(br_s.at[slot], br_r.at[slot], sibling)

    z_ids[0] = term_mid(0, x_ids[0])
    arrived(br_id[3], br_r.at[1])
    br_s[2] = (keep_br[...] + br_r[1].astype(F32)).astype(BF16)
    br_id[2] = send(br_s.at[2], br_r.at[2], across)
    z_ids[1] = term_mid(1, x_ids[1])
    g_ids[0] = term_sum(0, z_ids[0])
    arrived(ds_id[1], ds_r.at[0])
    arrived(ds_id[2], ds_r.at[2])

    def norm_back(j, term_gain):
        at = pl.ds(pl.multiple_of(j * height, height), height)
        d_scaled = own_ds[at, :]
        for r in (0, 2):
            d_scaled = d_scaled + ds_r[r, at, :].astype(F32)
        unit = normed[at, :]
        both = d_scaled * unit
        g = d_scaled * gain
        mean_g = jnp.mean(g, axis=-1, keepdims=True)
        mean_gn = jnp.mean(g * unit, axis=-1, keepdims=True)
        dpad[j, TOP : TOP + height, :] = (g - mean_g - unit * mean_gn) * rstd_ref[at, 0:1]
        return term_gain + jnp.sum(both.reshape(height // 8, 8, channels), axis=0)

    term_gain = lax.fori_loop(0, width, norm_back, jnp.zeros((8, channels), F32))
    z_ids[2] = term_mid(2, x_ids[2])

    def adjoint(columns):
        @pl.loop(0, channels // 128)
        def _(g):
            lanes = lanes_of(g)
            total = {c: jnp.zeros((height, 128), F32) for c in columns}
            for a in range(7):
                first = TOP + 3 - a
                shifted = [dpad[j, first : first + height, lanes] for j in range(width)]
                for b in range(7):
                    tap = kern_ref[pl.ds(7 * a + b, 1), lanes]
                    for j in range(width):
                        if j + b in total:
                            total[j + b] = total[j + b] + shifted[j] * tap
            for c in columns:
                core[c, :, lanes] = total[c]

    kfull[3] = jnp.zeros((16, channels), F32)
    kfull[3, 1:2, :] = jnp.sum(term_gain, axis=0, keepdims=True)
    g_ids[1] = term_sum(1, z_ids[1])
    z_ids[3] = term_mid(3, x_ids[3])

    def tap_sums(first_group, last_group):
        @pl.loop(first_group, last_group)
        def _(g):
            lanes = lanes_of(g)
            d_here = dpad[:, TOP : TOP + height, lanes]
            for a in range(7):
                shifted = ext[:, TOP - 3 + a : TOP - 3 + a + height, lanes]
                for b in range(7):
                    tap = 7 * a + b
                    both = (d_here * shifted[b : b + width]).reshape(cells // 8, 8, 128)
                    column = jnp.sum(jnp.sum(both, axis=0), axis=0, keepdims=True)
                    kfull[tap // 16, tap % 16 : tap % 16 + 1, lanes] = column

    tap_sums(0, channels // 256)
    term_spread(0, g_ids[0])
    g_ids[2] = term_sum(2, z_ids[2])
    tap_sums(channels // 256, channels // 128)
    kr_id = [None] + [
        send(kfull.at[f_peer[r]], kr.at[r - 1], {"fsdp": f_peer[r]}) for r in (1, 2, 3)
    ]
    term_spread(1, g_ids[1])
    g_ids[3] = term_sum(3, z_ids[3])

    adjoint([0, 1, 2, width + 3, width + 4, width + 5])
    for side, first in ((0, 0), (1, width + 3)):
        pick = picker(-seam_ref[0, side])
        for j in range(3):
            adj_s[side, rows_of(j), :] = dot(pick, core[first + j].astype(BF16)).astype(BF16)
    adj_w = send(adj_s.at[0], adj_r.at[1], {"tile": west})
    adj_e = send(adj_s.at[1], adj_r.at[0], {"tile": east})

    adjoint(list(range(3, width + 3)))

    total = kfull[f]
    for r in (1, 2, 3):
        arrived(kr_id[r], kr.at[r - 1])
        total = total + kr[r - 1]
    kl[...] = total
    kl_id = send(kl, klr, {"tile": x_peer})
    term_spread(2, g_ids[2])
    term_end(0)
    arrived(kl_id, klr)
    kz[z] = kl[...] + klr[...]
    kz_id = [None] + [send(kz.at[z], kz.at[z], {"tile": z_peer[r]}) for r in range(1, hi)]
    term_spread(3, g_ids[3])

    arrived(adj_w, adj_r.at[1])
    arrived(adj_e, adj_r.at[0])
    for j in range(width):
        value = cot_all[0, rows_of(j), :].astype(F32) + core[3 + j]
        if j < 3:
            value = value + adj_r[0, rows_of(j), :].astype(F32)
        if j >= width - 3:
            value = value + adj_r[1, rows_of(j - width + 3), :].astype(F32)
        put_column(flip, j, value)
    gather_lanes(flip, fgrad_ref)
    store(fgrad_ref, fgrad_hbm)

    for r in range(1, hi):
        arrived(kz_id[r], kz.at[z_from[r]])
    total = kz[0]
    for at in range(1, hi):
        total = total + kz[at]
    kf[f] = total * factor
    kf_id = [None] + [send(kf.at[f], kf.at[f], {"fsdp": f_peer[r]}) for r in (1, 2, 3)]

    term_end(1)
    arrived(br_id[1], br_r.at[0])
    arrived(br_id[2], br_r.at[2])
    for j in range(width):
        at = rows_of(j)
        value = ext[3 + j, TOP : TOP + height, :] + own_br[at, :]
        for r in (0, 2):
            value = value + br_r[r, at, :].astype(F32)
        put_column(flip2, j, value)
    gather_lanes(flip2, mixed_ref)
    store(mixed_ref, mixed_hbm)

    term_end(2)
    for r in (1, 2, 3):
        arrived(kf_id[r], kf.at[f_peer[r]])
    for at in range(3):
        kgrad_ref[16 * at : 16 * at + 16, :] = kf[at]
    kgrad_ref[48:49, :] = kf[3, 0:1, :]
    ggrad_ref[...] = kf[3, 1:2, :]
    store(kgrad_ref, kgrad_hbm)
    store(ggrad_ref, ggrad_hbm)

    term_end(3)
    for copy in stores:
        copy.wait()
    for copy in started:
        copy.wait_send()
    assert len(started) <= n_sems


def write_out(*refs):
    sources, targets, held, wide = refs[:5], refs[5:11], refs[11:16], refs[16:18]
    in_sems, out_sems = refs[18:]
    order = list(range(4))
    loads = [pltpu.make_async_copy(sources[i], held[i], in_sems.at[i]) for i in order]
    terms = [
        pltpu.make_async_copy(sources[4].at[h], held[4].at[h], in_sems.at[4 + h])
        for h in range(4)
    ]
    for load in terms + loads:
        load.start()
    stores = []

    def save(src, dst):
        stores.append(pltpu.make_async_copy(src, dst, out_sems.at[len(stores)]))
        stores[-1].start()

    _, sides, hi, piece, half = held[4].shape
    for h in range(4):
        terms[h].wait()
        which = 1 - h // 2
        for side in range(sides):
            first = ((h % 2) * 2 + side) * half
            wide[which][:, first : first + half] = (
                held[4][h, side].astype(F32).reshape(hi * piece, half)
            )
        if h % 2 == 1:
            save(wide[which], targets[4 + which])
    for i in order:
        loads[i].wait()
        save(held[i], targets[i])
    for copy in stores:
        copy.wait()


def body(tiles, shards, fields, seam_shift, kernel, gain, w_in, w_out, cotangent):
    _, height, width, channels = fields.shape
    cells = height * width
    hidden = w_in.shape[1]
    assert shards == 4 and tiles % 2 == 0 and kernel.shape[0] == 49
    assert hidden == channels and channels % (16 * (tiles // 2)) == 0
    hi = tiles // 2
    factor = 1.0 / math.sqrt(cells * tiles * shards)
    half = channels // 4
    piece = channels // hi
    n_sems = 32 + 4 * (1 + 2 * (hi - 1) + hi) + hi
    padded = height + 16

    def vmem(shape, kind):
        return pltpu.VMEM(shape, kind)

    away = pl.BlockSpec(memory_space=pltpu.HBM)
    rows = (cells, channels)
    outs = pl.pallas_call(
        functools.partial(kernel_body, tiles, hi, height, width, channels, factor, n_sems),
        out_shape=(
            jax.ShapeDtypeStruct(rows, BF16),
            jax.ShapeDtypeStruct(rows, BF16),
            jax.ShapeDtypeStruct(kernel.shape, F32),
            jax.ShapeDtypeStruct((1, channels), F32),
            jax.ShapeDtypeStruct((4, 2, hi, piece, half), BF16),
        ),
        in_specs=[
            away, pl.BlockSpec(memory_space=pltpu.SMEM), away, away, away, away, away,
        ],
        out_specs=[away] * 5,
        scratch_shapes=[
            vmem((width + 6, padded, channels), F32),
            vmem((width, padded, channels), F32),
            vmem((channels // 128, cells, 128), F32),
            vmem((channels // 128, cells, 128), F32),
            vmem(rows, F32),
            vmem(rows, F32),
            vmem((cells, 128), F32),
            vmem(rows, F32),
            vmem(rows, F32),
            vmem(rows, F32),
            vmem(rows, F32),
            vmem((4, cells, hidden), BF16),
            vmem((4, cells, hidden), BF16),
            vmem((2, cells, hidden), F32),
            vmem((hidden, 4 * cells), BF16),
            vmem((channels, 4 * cells), BF16),
            vmem((hidden, channels), BF16),
            vmem((channels, hidden), BF16),
            vmem((cells, hidden), F32),
            vmem((cells, hidden), F32),
            vmem((2, 3 * height, channels), BF16),
            vmem((2, 3 * height, channels), BF16),
            vmem((2, 3 * height, channels), BF16),
            vmem((2, 3 * height, channels), BF16),
            vmem((width + 6, height, channels), F32),
            vmem((4, cells, channels), BF16),
            vmem((4, cells, channels), BF16),
            vmem((3, cells, channels), BF16),
            vmem((3, cells, channels), BF16),
            vmem((3, cells, channels), BF16),
            vmem((3, cells, channels), BF16),
            vmem((4, 2, channels, half), F32),
            vmem((4, 2, channels, half), BF16),
            vmem((4, channels, half), BF16),
            vmem((4, channels, half), F32),
            vmem((4, hi, piece, half), BF16),
            vmem((4, hi, piece, half), BF16),
            vmem((4, hi, piece, half), BF16),
            vmem((4, hi, piece, half), BF16),
            vmem((4, 16, channels), F32),
            vmem((3, 16, channels), F32),
            vmem((16, channels), F32),
            vmem((16, channels), F32),
            vmem((hi, 16, channels), F32),
            vmem((4, 16, channels), F32),
            vmem(rows, BF16),
            vmem(kernel.shape, F32),
            vmem((1, channels), F32),
            vmem(w_in.shape, BF16),
            vmem(w_out.shape, BF16),
            vmem(rows, BF16),
            vmem(rows, BF16),
            vmem(rows, BF16),
            vmem(kernel.shape, F32),
            vmem((1, channels), F32),
            pltpu.SemaphoreType.DMA((6,)),
            pltpu.SemaphoreType.DMA((12,)),
            pltpu.SemaphoreType.DMA((n_sems,)),
            pltpu.SemaphoreType.DMA((n_sems,)),
        ],
        compiler_params=pltpu.CompilerParams(
            collective_id=0, has_side_effects=True, vmem_limit_bytes=58 * 1024 * 1024
        ),
        name="block",
    )(
        fields.reshape(rows), seam_shift, kernel, gain.reshape(1, channels), w_in, w_out,
        cotangent.reshape(rows),
    )
    outs = pl.pallas_call(
        write_out,
        out_shape=[jax.ShapeDtypeStruct(out.shape, out.dtype) for out in outs[:4]]
        + [jax.ShapeDtypeStruct(w.shape, F32) for w in (w_in, w_out)],
        in_specs=[away] * 5,
        out_specs=[away] * 6,
        scratch_shapes=[pltpu.VMEM(out.shape, out.dtype) for out in outs]
        + [pltpu.VMEM(w.shape, F32) for w in (w_in, w_out)]
        + [pltpu.SemaphoreType.DMA((8,)), pltpu.SemaphoreType.DMA((6,))],
        compiler_params=pltpu.CompilerParams(vmem_limit_bytes=58 * 1024 * 1024),
        name="write_out",
    )(*outs)
    mixed, field_grad, kernel_grad, gain_grad, w_in_grad, w_out_grad = outs
    return (
        mixed.reshape(fields.shape), field_grad.reshape(fields.shape), kernel_grad,
        gain_grad.reshape(channels), w_in_grad, w_out_grad,
    )


def solution(mesh):
    return jax.shard_map(
        functools.partial(body, mesh.shape["tile"], mesh.shape["fsdp"]),
        mesh=mesh,
        in_specs=(
            P("fsdp", None, "tile", None),
            P("tile", None),
            P(),
            P(),
            P(None, "fsdp"),
            P("fsdp", None),
            P("fsdp", None, "tile", None),
        ),
        out_specs=(
            P("fsdp", None, "tile", None),
            P("fsdp", None, "tile", None),
            P(),
            P(),
            P(None, "fsdp"),
            P("fsdp", None),
        ),
        check_vma=False,
    )
```
